256 devices in a mesh: chan: 8 (over z_lo, core), bl: 32 (over y, z_hi, x).
Axes of the slice: x: 4, y: 4, z: 8 (z_hi: 2, z_lo: 4; z = z_hi * 4 + z_lo), core: 2. Of those that a mesh axis runs over, the one named last changes fastest.
Arguments:
- visibility: bfloat16 [2, 1024, 1024], P(None, ('chan', 'bl')), may hold values from -6 to 6
- weights: bfloat16 [1024, 1024], P(('chan', 'bl')), may hold values from 0.25 to 1
- positions: float32 [2, 512], replicated, may hold values from -96 to 96
- station_pairs: int32 [2, 1024], P(None, ('chan', 'bl')), may hold values from 0 to 511
- facet_shift: int32 [2, 2], replicated, may hold values from -512 to 512
Outputs:
- subband_images: float32 [8, 512, 1024], P('chan', 'bl')
The draws below stay inside these ranges and needn't reach their ends.
All inputs are finite; a program needn't handle non-finite values.
Results may differ from the reference program's by a relative error of at most 0.0037.
Values may be sent and summed in bfloat16 or wider, within the bound.
No kernel may reach another device: no remote copies, remote signals or barrier semaphores. Data moves between devices by JAX's collectives and lax.ppermute only.
A program may use at most 64 MiB of HBM per device.

```python
import math
import jax
import jax.numpy as jnp
from jax import lax

PIX = 512
FACETS = 2
STATION_COUNT = 512
GROUP_CHANNELS = 128
CHANNEL_TOTAL = 1024
BASELINE_TOTAL = 1024
N_CHAN = 8


def set_ends(drawn, stream_key, low, largest):
    shape = drawn.shape
    place = [jax.random.randint(jax.random.fold_in(stream_key, axis), (), 0, shape[axis]) for axis in range(len(shape))]
    drawn = drawn.at[tuple(place)].set(low)
    longest = shape.index(max(shape))
    place[longest] = (place[longest] + 1) % shape[longest]
    return drawn.at[tuple(place)].set(largest)


def block_levels(rng, dims, shards, smallest, high):
    def one(position, parts):
        steps = jax.random.uniform(jax.random.fold_in(jax.random.fold_in(rng, 6), position), (parts,), jnp.float32, smallest / len(shards), high / len(shards))
        return jnp.repeat(jnp.exp(steps), dims[position] // parts).reshape((-1,) + (1,) * (len(dims) - position - 1))

    factor_of = one(*shards[0])
    for cut in shards[1:]:
        factor_of = factor_of * one(*cut)
    return factor_of


def noise(key, extent, scale, limit, pieces=(), held_as=jnp.bfloat16):
    gain = block_levels(key, extent, pieces, -0.22, 0.18) if pieces else 1.0
    values = jax.random.normal(key, extent, jnp.float32) * scale * gain
    return jnp.minimum(jnp.maximum(values, -limit), limit).astype(held_as)


def setup_inputs(seed: int = 0) -> dict:
    seeds = jax.random.split(jax.random.key(seed), 6)
    visibility = noise(seeds[0], (2, BASELINE_TOTAL, CHANNEL_TOTAL), 1.0, 6.0, ((1, 256),))
    weights = jnp.clip(jnp.exp(math.log(1.0) - 1.3862944 * jax.random.uniform(seeds[1], (BASELINE_TOTAL, CHANNEL_TOTAL), jnp.float32) ** block_levels(seeds[1], (BASELINE_TOTAL, CHANNEL_TOTAL), ((0, 256),), -0.2, 0.2)), 0.25, 1.0).astype(jnp.bfloat16)
    positions = jnp.clip(jax.random.uniform(seeds[2], (2, STATION_COUNT), jnp.float32, -96.0, 96.0), -96.0, 96.0)
    station_pairs = set_ends(jax.random.randint(seeds[3], (2, BASELINE_TOTAL), 0, STATION_COUNT), jax.random.fold_in(seeds[3], 1), 0, STATION_COUNT - 1).astype(jnp.int32)
    facet_shift = set_ends(jax.random.randint(seeds[4], (2, FACETS), -PIX, PIX + 1), jax.random.fold_in(seeds[4], 1), -PIX, PIX).astype(jnp.int32)
    return dict(visibility=visibility, weights=weights, positions=positions, station_pairs=station_pairs, facet_shift=facet_shift)


two_pi = 2.0 * math.pi

def rounded(values):
    narrow = lax.optimization_barrier(values.astype(jnp.bfloat16))
    return narrow.astype(jnp.float32)

def reference(visibility, weights, positions, station_pairs, facet_shift):
    east_span = positions[0][station_pairs[0]] - positions[0][station_pairs[1]]
    north_span = positions[1][station_pairs[0]] - positions[1][station_pairs[1]]
    frequency = 1.0 + jnp.arange(CHANNEL_TOTAL, dtype=jnp.float32) / CHANNEL_TOTAL
    offsets = facet_shift.astype(jnp.float32)
    pixel_index = jnp.arange(PIX, dtype=jnp.float32)
    block_offset = math.gcd(BASELINE_TOTAL, max(1, 4096 // GROUP_CHANNELS))
    block_number = BASELINE_TOTAL // block_offset
    image_scale = 1.0 / math.sqrt(BASELINE_TOTAL * GROUP_CHANNELS)
    results = []
    for group in range(N_CHAN):
        low = group * GROUP_CHANNELS
        high = low + GROUP_CHANNELS
        freq_group = frequency[low:high]
        weight_group = weights[:, low:high].astype(jnp.float32)
        real_part = weight_group * visibility[0][:, low:high].astype(jnp.float32)
        imag_part = weight_group * visibility[1][:, low:high].astype(jnp.float32)
        east_turns = two_pi * (east_span[:, None] * freq_group[None, :])
        north_turns = two_pi * (north_span[:, None] * freq_group[None, :])
        blocked = tuple((values.reshape(block_number, block_offset * GROUP_CHANNELS) for values in (real_part, imag_part, east_turns, north_turns)))
        facet_images = []
        for facet in range(FACETS):
            left_coord = (offsets[0, facet] + pixel_index - PIX // 2) / PIX
            right_coord = (offsets[1, facet] + pixel_index - PIX // 2) / PIX

            def accumulate(total, block):
                real_blk, imag_blk, east_blk, north_blk = block
                angle_left = east_blk[:, None] * left_coord[None, :]
                cos_left = jnp.cos(angle_left)
                sin_left = jnp.sin(angle_left)
                left_real = rounded(real_blk[:, None] * cos_left - imag_blk[:, None] * sin_left)
                left_imag = rounded(real_blk[:, None] * sin_left + imag_blk[:, None] * cos_left)
                angle_right = north_blk[:, None] * right_coord[None, :]
                cos_right = rounded(jnp.cos(angle_right))
                sin_right = rounded(jnp.sin(angle_right))
                total = total + jnp.dot(left_real.T, cos_right, precision=lax.Precision.HIGHEST)
                total = total - jnp.dot(left_imag.T, sin_right, precision=lax.Precision.HIGHEST)
                return (total, None)
            image, _ = lax.scan(accumulate, jnp.zeros((PIX, PIX), jnp.float32), blocked)
            facet_images.append(image * image_scale)
        results.append(jnp.concatenate(facet_images, axis=1))
    return jnp.stack(results)
```

```python
import functools
import math

import jax
import jax.numpy as jnp
from jax import lax
from jax.experimental import pallas as pl
from jax.experimental.pallas import tpu as pltpu
from jax.sharding import Mesh, PartitionSpec as P

PIX = 512
HALF = PIX // 2
FACETS = 2
CHANNELS = 1024
GROUPS = 8
LANES = 128
READ_ROWS = 4
RUN_ROWS = 64
RUNS = 4
STEPS = RUN_ROWS // 8
HALVES = 2
SOURCES = GROUPS * HALVES
BLOCKS = SOURCES * READ_ROWS
CHUNK_BLOCKS = 8
CHUNK = CHUNK_BLOCKS * LANES
CHUNKS = BLOCKS // CHUNK_BLOCKS
PEERS = 16
OUT_ROWS = 16
COS_COEF = (
    1.0, -19.739208221435547, 64.93939208984375, -85.45665740966797,
    60.242130279541016, -26.4046688079834, 7.800131797790527, -1.4531123638153076,
)
SIN_COEF = (
    6.2831854820251465, -41.34170150756836, 81.60513305664062, -76.70301818847656,
    42.02592849731445, -14.899847984313965, 3.238137722015381,
)


def poly(coef, z):
    total = jnp.full_like(z, coef[-1])
    for c in coef[-2::-1]:
        total = total * z + c
    return total


def frac(turns):
    return turns - jnp.floor(turns + 0.5)


def cos_sin_reduced(r):
    z = r * r
    return poly(COS_COEF, z), poly(SIN_COEF, z) * r


def cos_sin(turns):
    return cos_sin_reduced(frac(turns))


def pack_kernel(vis_ref, weight_ref, pos_ref, pair_ref, out_ref):
    weight = weight_ref[...].astype(jnp.float32)
    real = weight * vis_ref[0].astype(jnp.float32)
    imag = weight * vis_ref[1].astype(jnp.float32)
    shape = (READ_ROWS, CHANNELS)
    channel = lax.broadcasted_iota(jnp.int32, shape, 1).astype(jnp.float32)
    frequency = 1.0 + channel / CHANNELS
    row = lax.broadcasted_iota(jnp.int32, shape, 0)
    spans = []
    for axis in range(2):
        span = jnp.zeros(shape, jnp.float32)
        for b in range(READ_ROWS):
            value = pos_ref[axis, pair_ref[0, b]] - pos_ref[axis, pair_ref[1, b]]
            span = jnp.where(row == b, value, span)
        spans.append(span * frequency)
    for a, values in enumerate((real, imag, *spans)):
        for g in range(GROUPS):
            part = values[:, g * LANES : (g + 1) * LANES]
            for h in range(HALVES):
                out_ref[g * HALVES + h, a * READ_ROWS : (a + 1) * READ_ROWS, :] = part


(V0R, V0I, V1R, V1I, EAST, NORTH, C8E, S8E, C128E, S128E, C8N, S8N, C64N, S64N, TABLE) = range(15)


def image_kernel(half_ref, shift_ref, data_ref, out_ref, table, acc, *slots):
    for s in range(SOURCES):
        for a, t in enumerate((V0R, V0I, EAST, NORTH)):
            table[t, s * READ_ROWS : (s + 1) * READ_ROWS, :] = data_ref[
                s, a * READ_ROWS : (a + 1) * READ_ROWS, :
            ]
    base_row = half_ref[0] * RUN_ROWS - HALF

    def prepare(i, carry):
        rows = pl.ds(pl.multiple_of(i * 8, 8), 8)
        east = table[EAST, rows, :]
        north = table[NORTH, rows, :]
        real = table[V0R, rows, :]
        imag = table[V0I, rows, :]
        for f in range(FACETS):
            left = (shift_ref[0, f] + base_row).astype(jnp.float32) * (1.0 / PIX)
            right = (shift_ref[1, f].astype(jnp.float32) - 0.5) * (1.0 / PIX)
            cos, sin = cos_sin(frac(east * left) + frac(north * right))
            table[V0R + 2 * f, rows, :] = real * cos - imag * sin
            table[V0I + 2 * f, rows, :] = real * sin + imag * cos
        for t, turns in (
            (C8E, east * (8.0 / PIX)),
            (C128E, east * (128.0 / PIX)),
            (C8N, north * (8.0 / PIX)),
            (C64N, north * (64.0 / PIX)),
        ):
            cos, sin = cos_sin(turns)
            table[t, rows, :] = cos
            table[t + 1, rows, :] = sin
        return carry

    lax.fori_loop(0, BLOCKS // 8, prepare, 0)

    lane_row = lax.broadcasted_iota(jnp.int32, (8, LANES), 0).astype(jnp.float32)

    def rotate(u, turn):
        (ur, ui), (c, s) = u, turn
        return ur * c - ui * s, ur * s + ui * c

    def generate(first_block, slot):
        left_re, left_im, right_re, right_im = slot
        for t in range(CHUNK_BLOCKS):
            block = first_block + t
            lanes = slice(t * LANES, (t + 1) * LANES)

            def row(i):
                return jnp.broadcast_to(table[i, pl.ds(block, 1), :], (8, LANES))

            def emit(refs, first_row, stride, start, turn_run, turn_step):
                anchors = [(start, rotate(start, turn_step))]
                anchors.append(tuple(rotate(u, turn_run) for u in anchors[0]))
                twice_run = 2.0 * turn_run[0]
                for _ in range(RUNS - 2):
                    anchors.append(
                        tuple(
                            tuple(twice_run * b - a for a, b in zip(old, new))
                            for old, new in zip(anchors[-2], anchors[-1])
                        )
                    )
                twice = 2.0 * turn_step[0]
                for r, (first, second) in enumerate(anchors):
                    for part, ref in enumerate(refs):
                        before, now = first[part], second[part]
                        for j in range(0, STEPS, 2):
                            if j:
                                before = twice * now - before
                                now = twice * before - now
                            at = first_row + r * stride + j * 8
                            ref[at : at + 16, lanes] = jnp.concatenate(
                                [before, now], axis=0
                            ).astype(jnp.bfloat16)

            base = cos_sin(row(EAST) * (lane_row * (1.0 / PIX)))
            turn_run = (row(C128E), row(S128E))
            turn_step = (row(C8E), row(S8E))
            for f in range(FACETS):
                start = rotate(base, (row(V0R + 2 * f), row(V0I + 2 * f)))
                emit((left_re, left_im), f * HALF, RUN_ROWS, start, turn_run, turn_step)
            start = cos_sin(row(NORTH) * ((lane_row + 0.5) * (1.0 / PIX)))
            emit(
                (right_re, right_im), 0, RUN_ROWS, start,
                (row(C64N), row(S64N)), (row(C8N), row(S8N)),
            )

    def multiply(slot):
        left_re, left_im, right_re, right_im = slot
        contract = (((1,), (1,)), ((), ()))
        for i, (left, right) in enumerate(((left_re, right_re), (left_im, right_im))):
            acc[i] += lax.dot_general(
                left[...], right[...], contract, preferred_element_type=jnp.float32
            )

    slot_a, slot_b = slots[:4], slots[4:]
    acc[...] = jnp.zeros_like(acc)
    generate(0, slot_a)

    def step(i, carry):
        first = i * (2 * CHUNK_BLOCKS)
        generate(first + CHUNK_BLOCKS, slot_b)
        multiply(slot_a)
        generate(lax.rem(first + 2 * CHUNK_BLOCKS, BLOCKS), slot_a)
        multiply(slot_b)
        return carry

    lax.fori_loop(0, CHUNKS // 2, step, 0)
    for f in range(FACETS):
        for i in range(2):
            column = (f * 2 + i) * HALF
            out_ref[:, column : column + HALF] = acc[i, f * HALF : (f + 1) * HALF].astype(
                jnp.bfloat16
            )


def combine_kernel(scale, data_ref, out_ref):
    total = data_ref[0].astype(jnp.float32)
    for i in range(1, PEERS):
        total = total + data_ref[i].astype(jnp.float32)
    total = total * scale
    flip = (
        lax.broadcasted_iota(jnp.int32, (HALF, HALF), 0)
        + lax.broadcasted_iota(jnp.int32, (HALF, HALF), 1)
        == HALF - 1
    ).astype(jnp.bfloat16)
    for f in range(FACETS):
        even = total[:, f * PIX : f * PIX + HALF]
        odd = total[:, f * PIX + HALF : (f + 1) * PIX]
        rest = even + odd
        mirrored = jnp.zeros_like(rest)
        for _ in range(3):
            part = rest.astype(jnp.bfloat16)
            rest = rest - part.astype(jnp.float32)
            mirrored = mirrored + jnp.dot(part, flip, preferred_element_type=jnp.float32)
        out_ref[0, :, f * PIX : f * PIX + HALF] = mirrored
        out_ref[0, :, f * PIX + HALF : (f + 1) * PIX] = even - odd


VMEM = pl.BlockSpec(memory_space=pltpu.VMEM)
SMEM = pl.BlockSpec(memory_space=pltpu.SMEM)


def pack(visibility, weights, positions, station_pairs):
    return pl.pallas_call(
        pack_kernel,
        out_shape=jax.ShapeDtypeStruct((SOURCES, 4 * READ_ROWS, LANES), jnp.float32),
        in_specs=[VMEM, VMEM, SMEM, SMEM],
        out_specs=VMEM,
        name="pack",
    )(visibility, weights, positions, station_pairs)


def make_images(half, facet_shift, arrived):
    slot = [
        pltpu.VMEM((FACETS * HALF, CHUNK), jnp.bfloat16),
        pltpu.VMEM((FACETS * HALF, CHUNK), jnp.bfloat16),
        pltpu.VMEM((HALF, CHUNK), jnp.bfloat16),
        pltpu.VMEM((HALF, CHUNK), jnp.bfloat16),
    ]
    return pl.pallas_call(
        image_kernel,
        out_shape=jax.ShapeDtypeStruct((HALF, FACETS * PIX), jnp.bfloat16),
        in_specs=[SMEM, SMEM, VMEM],
        out_specs=VMEM,
        scratch_shapes=[
            pltpu.VMEM((TABLE, BLOCKS, LANES), jnp.float32),
            pltpu.VMEM((2, FACETS * HALF, HALF), jnp.float32),
            *slot,
            *slot,
        ],
        compiler_params=pltpu.CompilerParams(vmem_limit_bytes=40 * 1024 * 1024),
        name="images",
    )(half, facet_shift, arrived)


def combine(scale, parts):
    return pl.pallas_call(
        functools.partial(combine_kernel, scale),
        out_shape=jax.ShapeDtypeStruct((1, OUT_ROWS, FACETS * PIX), jnp.float32),
        in_specs=[VMEM],
        out_specs=VMEM,
        name="combine",
    )(parts)


def body(visibility, weights, positions, station_pairs, facet_shift):
    packed = pack(visibility, weights, positions, station_pairs)
    arrived = lax.all_to_all(packed, ("chan", "zh"), split_axis=0, concat_axis=0, tiled=True)
    half = lax.axis_index("zh").astype(jnp.int32).reshape(1)
    images = make_images(half, facet_shift, arrived)
    parts = lax.all_to_all(
        images.reshape(PEERS, OUT_ROWS, FACETS * PIX),
        ("y", "x"), split_axis=0, concat_axis=0, tiled=True,
    )
    scale = 1.0 / math.sqrt(READ_ROWS * GROUPS * 32 * LANES)
    return combine(scale, parts)


def solution(mesh):
    fine = Mesh(mesh.devices.reshape(GROUPS, 4, HALVES, 4), ("chan", "y", "zh", "x"))
    line = ("y", "zh", "x")
    in_specs = (
        P(None, ("chan", *line), None),
        P(("chan", *line), None),
        P(),
        P(None, ("chan", *line)),
        P(),
    )
    out_specs = P("chan", line, None)
    return jax.shard_map(body, mesh=fine, in_specs=in_specs, out_specs=out_specs, check_vma=False)
```

```python
import functools
import math

import jax
import jax.numpy as jnp
from jax import lax
from jax.experimental import pallas as pl
from jax.experimental.pallas import tpu as pltpu
from jax.sharding import Mesh, PartitionSpec as P

PIX = 512
HALF = PIX // 2
FACETS = 2
CHANNELS = 1024
GROUPS = 8
LANES = 128
READ_ROWS = 4
RUN_ROWS = 64
RUNS = 4
STEPS = RUN_ROWS // 8
RUN_HALF = RUN_ROWS // 2
HALVES = 2
SOURCES = GROUPS * HALVES
BLOCKS = SOURCES * READ_ROWS
CHUNK_BLOCKS = 4
CHUNK = CHUNK_BLOCKS * LANES
CHUNKS = BLOCKS // CHUNK_BLOCKS
PEERS = 16
OUT_ROWS = 16
COS_COEF = (
    1.0, -19.739208221435547, 64.93939208984375, -85.45665740966797,
    60.242130279541016, -26.4046688079834, 7.800131797790527, -1.4531123638153076,
)
SIN_COEF = (
    6.2831854820251465, -41.34170150756836, 81.60513305664062, -76.70301818847656,
    42.02592849731445, -14.899847984313965, 3.238137722015381,
)


def poly(coef, z):
    total = jnp.full_like(z, coef[-1])
    for c in coef[-2::-1]:
        total = total * z + c
    return total


def frac(turns):
    return turns - jnp.floor(turns + 0.5)


def cos_sin_reduced(r):
    z = r * r
    return poly(COS_COEF, z), poly(SIN_COEF, z) * r


def cos_sin(turns):
    return cos_sin_reduced(frac(turns))


def pack_kernel(vis_ref, weight_ref, pos_ref, pair_ref, out_ref):
    weight = weight_ref[...].astype(jnp.float32)
    real = weight * vis_ref[0].astype(jnp.float32)
    imag = weight * vis_ref[1].astype(jnp.float32)
    shape = (READ_ROWS, CHANNELS)
    channel = lax.broadcasted_iota(jnp.int32, shape, 1).astype(jnp.float32)
    frequency = 1.0 + channel / CHANNELS
    row = lax.broadcasted_iota(jnp.int32, shape, 0)
    spans = []
    for axis in range(2):
        span = jnp.zeros(shape, jnp.float32)
        for b in range(READ_ROWS):
            value = pos_ref[axis, pair_ref[0, b]] - pos_ref[axis, pair_ref[1, b]]
            span = jnp.where(row == b, value, span)
        spans.append(span * frequency)
    for a, values in enumerate((real, imag, *spans)):
        for g in range(GROUPS):
            part = values[:, g * LANES : (g + 1) * LANES]
            for h in range(HALVES):
                out_ref[g * HALVES + h, a * READ_ROWS : (a + 1) * READ_ROWS, :] = part


PHASED = 0
EAST, NORTH, C8E, S8E, C8N, S8N, C64N, S64N, TABLE = range(2 * FACETS * RUNS, 2 * FACETS * RUNS + 9)


def rotate(u, turn):
    (ur, ui), (c, s) = u, turn
    return ur * c - ui * s, ur * s + ui * c


def image_kernel(half_ref, shift_ref, data_ref, out_ref, table, acc, *slots):
    for s in range(SOURCES):
        for a, t in enumerate((PHASED, PHASED + 1, EAST, NORTH)):
            table[t, s * READ_ROWS : (s + 1) * READ_ROWS, :] = data_ref[
                s, a * READ_ROWS : (a + 1) * READ_ROWS, :
            ]
    base_row = (half_ref[0] * RUN_ROWS - HALF).astype(jnp.float32) + (RUN_HALF - 0.5)

    def prepare(i, carry):
        rows = pl.ds(pl.multiple_of(i * 8, 8), 8)
        east = table[EAST, rows, :]
        north = table[NORTH, rows, :]
        seen = table[PHASED, rows, :], table[PHASED + 1, rows, :]
        next_run = cos_sin(east * (2.0 * RUN_ROWS / PIX))
        for f in range(FACETS):
            left = (shift_ref[0, f].astype(jnp.float32) + base_row) * (1.0 / PIX)
            right = (shift_ref[1, f].astype(jnp.float32) - 0.5) * (1.0 / PIX)
            phased = rotate(seen, cos_sin(frac(east * left) + frac(north * right)))
            for r in range(RUNS):
                if r:
                    phased = rotate(phased, next_run)
                at = PHASED + 2 * (f * RUNS + r)
                table[at, rows, :], table[at + 1, rows, :] = phased
        for t, turns in (
            (C8E, east * (8.0 / PIX)),
            (C8N, north * (8.0 / PIX)),
            (C64N, north * (64.0 / PIX)),
        ):
            cos, sin = cos_sin(turns)
            table[t, rows, :] = cos
            table[t + 1, rows, :] = sin
        return carry

    lax.fori_loop(0, BLOCKS // 8, prepare, 0)

    offsets = lax.broadcasted_iota(jnp.int32, (8, LANES), 0).astype(jnp.float32) + 0.5
    offsets = offsets * (1.0 / PIX)

    def generate(first_block, slot):
        left_cos, left_sin, right_cos, right_sin = slot
        for t in range(CHUNK_BLOCKS):
            block = first_block + t
            lanes = slice(t * LANES, (t + 1) * LANES)

            def row(i):
                return jnp.broadcast_to(table[i, pl.ds(block, 1), :], (8, LANES))

            def put(ref, at, first, second):
                ref[at : at + 16, lanes] = jnp.concatenate([first, second], axis=0).astype(
                    jnp.bfloat16
                )

            base = cos_sin(row(EAST) * offsets)
            turn = (row(C8E), row(S8E))
            wave = [base, rotate(base, turn)]
            twice = 2.0 * turn[0]
            for _ in range(2, RUN_HALF // 8):
                wave.append(tuple(twice * b - a for a, b in zip(wave[-2], wave[-1])))
            for f in range(FACETS):
                for r in range(RUNS):
                    index = PHASED + 2 * (f * RUNS + r)
                    real, imag = row(index), row(index + 1)
                    at = (f * RUNS + r) * RUN_HALF
                    for j in range(0, RUN_HALF // 8, 2):
                        (c0, s0), (c1, s1) = wave[j], wave[j + 1]
                        put(left_cos, at + j * 8, real * c0, real * c1)
                        put(left_cos, at + HALF + j * 8, imag * s0, imag * s1)
                        put(left_sin, at + j * 8, real * s0, real * s1)
                        put(left_sin, at + HALF + j * 8, imag * c0, imag * c1)

            start = cos_sin(row(NORTH) * offsets)
            turn = (row(C8N), row(S8N))
            next_run = (row(C64N), row(S64N))
            anchors = [(start, rotate(start, turn))]
            anchors.append(tuple(rotate(u, next_run) for u in anchors[0]))
            twice = 2.0 * next_run[0]
            for _ in range(2, RUNS):
                anchors.append(
                    tuple(
                        tuple(twice * b - a for a, b in zip(old, new))
                        for old, new in zip(anchors[-2], anchors[-1])
                    )
                )
            twice = 2.0 * turn[0]
            for r, (first, second) in enumerate(anchors):
                for part, ref in enumerate((right_cos, right_sin)):
                    before, now = first[part], second[part]
                    for j in range(0, STEPS, 2):
                        if j:
                            before = twice * now - before
                            now = twice * before - now
                        put(ref, r * RUN_ROWS + j * 8, before, now)

    def multiply(slot):
        left_cos, left_sin, right_cos, right_sin = slot
        contract = (((1,), (1,)), ((), ()))
        for i, (left, right) in enumerate(((left_cos, right_cos), (left_sin, right_sin))):
            acc[i] += lax.dot_general(
                left[...], right[...], contract, preferred_element_type=jnp.float32
            )

    slot_a, slot_b = slots[:4], slots[4:]
    acc[...] = jnp.zeros_like(acc)
    generate(0, slot_a)

    def step(i, carry):
        first = i * (2 * CHUNK_BLOCKS)
        generate(first + CHUNK_BLOCKS, slot_b)
        multiply(slot_a)
        generate(lax.rem(first + 2 * CHUNK_BLOCKS, BLOCKS), slot_a)
        multiply(slot_b)
        return carry

    lax.fori_loop(0, CHUNKS // 2, step, 0)
    for f in range(FACETS):
        for r in range(RUNS):
            at = (f * RUNS + r) * RUN_HALF
            for i in range(2):
                column = (f * 2 + i) * HALF
                for k in range(RUN_HALF // OUT_ROWS):
                    rows = slice(at + k * OUT_ROWS, at + (k + 1) * OUT_ROWS)
                    rows_imag = slice(at + HALF + k * OUT_ROWS, at + HALF + (k + 1) * OUT_ROWS)
                    a, b = acc[i, rows], acc[i, rows_imag]
                    below, above = (a - b, a + b) if i == 0 else (b + a, b - a)
                    for place, values in ((2 + k, below), (1 - k, above)):
                        out_ref[r * 4 + place, :, column : column + HALF] = values.astype(jnp.bfloat16)


def combine_kernel(scale, place_ref, data_ref, out_ref):
    shape = (OUT_ROWS, PEERS * OUT_ROWS)
    out_row = lax.broadcasted_iota(jnp.int32, shape, 0)
    sent_row = lax.broadcasted_iota(jnp.int32, shape, 1) % OUT_ROWS
    wanted = jnp.where(place_ref[0] < 2, OUT_ROWS - 1 - out_row, out_row)
    pick = (sent_row == wanted).astype(jnp.bfloat16)
    total = jnp.dot(pick, data_ref[...], preferred_element_type=jnp.float32) * scale
    flip = (
        lax.broadcasted_iota(jnp.int32, (HALF, HALF), 0)
        + lax.broadcasted_iota(jnp.int32, (HALF, HALF), 1)
        == HALF - 1
    ).astype(jnp.bfloat16)
    for f in range(FACETS):
        even = total[:, f * PIX : f * PIX + HALF]
        odd = total[:, f * PIX + HALF : (f + 1) * PIX]
        rest = even + odd
        mirrored = jnp.zeros_like(rest)
        for _ in range(3):
            part = rest.astype(jnp.bfloat16)
            rest = rest - part.astype(jnp.float32)
            mirrored = mirrored + jnp.dot(part, flip, preferred_element_type=jnp.float32)
        out_ref[0, :, f * PIX : f * PIX + HALF] = mirrored
        out_ref[0, :, f * PIX + HALF : (f + 1) * PIX] = even - odd


VMEM = pl.BlockSpec(memory_space=pltpu.VMEM)
SMEM = pl.BlockSpec(memory_space=pltpu.SMEM)


def pack(visibility, weights, positions, station_pairs):
    return pl.pallas_call(
        pack_kernel,
        out_shape=jax.ShapeDtypeStruct((SOURCES, 4 * READ_ROWS, LANES), jnp.float32),
        in_specs=[VMEM, VMEM, SMEM, SMEM],
        out_specs=VMEM,
        name="pack",
    )(visibility, weights, positions, station_pairs)


def make_images(half, facet_shift, arrived):
    slot = [
        pltpu.VMEM((FACETS * HALF, CHUNK), jnp.bfloat16),
        pltpu.VMEM((FACETS * HALF, CHUNK), jnp.bfloat16),
        pltpu.VMEM((HALF, CHUNK), jnp.bfloat16),
        pltpu.VMEM((HALF, CHUNK), jnp.bfloat16),
    ]
    return pl.pallas_call(
        image_kernel,
        out_shape=jax.ShapeDtypeStruct((PEERS, OUT_ROWS, FACETS * PIX), jnp.bfloat16),
        in_specs=[SMEM, SMEM, VMEM],
        out_specs=VMEM,
        scratch_shapes=[
            pltpu.VMEM((TABLE, BLOCKS, LANES), jnp.float32),
            pltpu.VMEM((2, FACETS * HALF, HALF), jnp.float32),
            *slot,
            *slot,
        ],
        compiler_params=pltpu.CompilerParams(vmem_limit_bytes=40 * 1024 * 1024),
        name="images",
    )(half, facet_shift, arrived)


def combine(scale, place, parts):
    return pl.pallas_call(
        functools.partial(combine_kernel, scale),
        out_shape=jax.ShapeDtypeStruct((1, OUT_ROWS, FACETS * PIX), jnp.float32),
        in_specs=[SMEM, VMEM],
        out_specs=VMEM,
        name="combine",
    )(place, parts.reshape(PEERS * OUT_ROWS, FACETS * PIX))


def body(visibility, weights, positions, station_pairs, facet_shift):
    packed = pack(visibility, weights, positions, station_pairs)
    arrived = lax.all_to_all(packed, ("chan", "zh"), split_axis=0, concat_axis=0, tiled=True)
    half = lax.axis_index("zh").astype(jnp.int32).reshape(1)
    images = make_images(half, facet_shift, arrived)
    parts = lax.all_to_all(
        images, ("y", "x"), split_axis=0, concat_axis=0, tiled=True
    )
    scale = 1.0 / math.sqrt(READ_ROWS * GROUPS * 32 * LANES)
    place = lax.axis_index("x").astype(jnp.int32).reshape(1)
    return combine(scale, place, parts)


def solution(mesh):
    fine = Mesh(mesh.devices.reshape(GROUPS, 4, HALVES, 4), ("chan", "y", "zh", "x"))
    line = ("y", "zh", "x")
    in_specs = (
        P(None, ("chan", *line), None),
        P(("chan", *line), None),
        P(),
        P(None, ("chan", *line)),
        P(),
    )
    out_specs = P("chan", line, None)
    return jax.shard_map(body, mesh=fine, in_specs=in_specs, out_specs=out_specs, check_vma=False)
```

```python
import functools
import math

import jax
import jax.numpy as jnp
from jax import lax
from jax.experimental import pallas as pl
from jax.experimental.pallas import tpu as pltpu
from jax.sharding import Mesh, PartitionSpec as P

PIX = 512
HALF = PIX // 2
FACETS = 2
CHANNELS = 1024
GROUPS = 8
LANES = 128
READ_ROWS = 4
RUN_ROWS = 64
RUNS = 4
STEPS = RUN_ROWS // 8
RUN_HALF = RUN_ROWS // 2
HALVES = 2
SOURCES = GROUPS * HALVES
BLOCKS = SOURCES * READ_ROWS
CHUNK_BLOCKS = 4
CHUNK = CHUNK_BLOCKS * LANES
CHUNKS = BLOCKS // CHUNK_BLOCKS
PEERS = 16
OUT_ROWS = 16
COS_COEF = (
    1.0, -19.739208221435547, 64.93939208984375, -85.45665740966797,
    60.242130279541016, -26.4046688079834, 7.800131797790527, -1.4531123638153076,
)
SIN_COEF = (
    6.2831854820251465, -41.34170150756836, 81.60513305664062, -76.70301818847656,
    42.02592849731445, -14.899847984313965, 3.238137722015381,
)


def poly(coef, z):
    total = jnp.full_like(z, coef[-1])
    for c in coef[-2::-1]:
        total = total * z + c
    return total


def frac(turns):
    return turns - jnp.floor(turns + 0.5)


def cos_sin_reduced(r):
    z = r * r
    return poly(COS_COEF, z), poly(SIN_COEF, z) * r


def cos_sin(turns):
    return cos_sin_reduced(frac(turns))


def pack_kernel(vis_ref, weight_ref, pos_ref, pair_ref, out_ref):
    weight = weight_ref[...].astype(jnp.float32)
    real = weight * vis_ref[0].astype(jnp.float32)
    imag = weight * vis_ref[1].astype(jnp.float32)
    shape = (READ_ROWS, CHANNELS)
    channel = lax.broadcasted_iota(jnp.int32, shape, 1).astype(jnp.float32)
    frequency = 1.0 + channel / CHANNELS
    row = lax.broadcasted_iota(jnp.int32, shape, 0)
    spans = []
    for axis in range(2):
        span = jnp.zeros(shape, jnp.float32)
        for b in range(READ_ROWS):
            value = pos_ref[axis, pair_ref[0, b]] - pos_ref[axis, pair_ref[1, b]]
            span = jnp.where(row == b, value, span)
        spans.append(span * frequency)
    for a, values in enumerate((real, imag, *spans)):
        for g in range(GROUPS):
            part = values[:, g * LANES : (g + 1) * LANES]
            for h in range(HALVES):
                out_ref[g * HALVES + h, a * READ_ROWS : (a + 1) * READ_ROWS, :] = part


PHASED = 0
EAST, NORTH, C8E, S8E, C8N, S8N, C64N, S64N, TABLE = range(2 * FACETS * RUNS, 2 * FACETS * RUNS + 9)


def rotate(u, turn):
    (ur, ui), (c, s) = u, turn
    return ur * c - ui * s, ur * s + ui * c


def image_kernel(half_ref, shift_ref, data_ref, out_ref, table, acc, *slots):
    for s in range(SOURCES):
        for a, t in enumerate((PHASED, PHASED + 1, EAST, NORTH)):
            table[t, s * READ_ROWS : (s + 1) * READ_ROWS, :] = data_ref[
                s, a * READ_ROWS : (a + 1) * READ_ROWS, :
            ]
    base_row = (half_ref[0] * RUN_ROWS - HALF).astype(jnp.float32) + (RUN_HALF - 0.5)

    def prepare(i, carry):
        rows = pl.ds(pl.multiple_of(i * 8, 8), 8)
        east = table[EAST, rows, :]
        north = table[NORTH, rows, :]
        seen = table[PHASED, rows, :], table[PHASED + 1, rows, :]
        next_run = cos_sin(east * (2.0 * RUN_ROWS / PIX))
        for f in range(FACETS):
            left = (shift_ref[0, f].astype(jnp.float32) + base_row) * (1.0 / PIX)
            right = (shift_ref[1, f].astype(jnp.float32) - 0.5) * (1.0 / PIX)
            phased = rotate(seen, cos_sin(frac(east * left) + frac(north * right)))
            for r in range(RUNS):
                if r:
                    phased = rotate(phased, next_run)
                at = PHASED + 2 * (f * RUNS + r)
                table[at, rows, :], table[at + 1, rows, :] = phased
        for t, turns in (
            (C8E, east * (8.0 / PIX)),
            (C8N, north * (8.0 / PIX)),
            (C64N, north * (64.0 / PIX)),
        ):
            cos, sin = cos_sin(turns)
            table[t, rows, :] = cos
            table[t + 1, rows, :] = sin
        return carry

    lax.fori_loop(0, BLOCKS // 8, prepare, 0, unroll=4)

    offsets = lax.broadcasted_iota(jnp.int32, (8, LANES), 0).astype(jnp.float32) + 0.5
    offsets = offsets * (1.0 / PIX)

    def generate(first_block, slot):
        left_cos, left_sin, right_cos, right_sin = slot
        for t in range(CHUNK_BLOCKS):
            block = first_block + t
            lanes = slice(t * LANES, (t + 1) * LANES)

            def row(i):
                return jnp.broadcast_to(table[i, pl.ds(block, 1), :], (8, LANES))

            def put(ref, at, first, second):
                ref[at : at + 16, lanes] = jnp.concatenate([first, second], axis=0).astype(
                    jnp.bfloat16
                )

            base = cos_sin(row(EAST) * offsets)
            turn = (row(C8E), row(S8E))
            wave = [base, rotate(base, turn)]
            twice = 2.0 * turn[0]
            for _ in range(2, RUN_HALF // 8):
                wave.append(tuple(twice * b - a for a, b in zip(wave[-2], wave[-1])))
            for f in range(FACETS):
                for r in range(RUNS):
                    index = PHASED + 2 * (f * RUNS + r)
                    real, imag = row(index), row(index + 1)
                    at = (f * RUNS + r) * RUN_HALF
                    for j in range(0, RUN_HALF // 8, 2):
                        (c0, s0), (c1, s1) = wave[j], wave[j + 1]
                        put(left_cos, at + j * 8, real * c0, real * c1)
                        put(left_cos, at + HALF + j * 8, imag * s0, imag * s1)
                        put(left_sin, at + j * 8, real * s0, real * s1)
                        put(left_sin, at + HALF + j * 8, imag * c0, imag * c1)

            start = cos_sin(row(NORTH) * offsets)
            turn = (row(C8N), row(S8N))
            next_run = (row(C64N), row(S64N))
            anchors = [(start, rotate(start, turn))]
            anchors.append(tuple(rotate(u, next_run) for u in anchors[0]))
            twice = 2.0 * next_run[0]
            for _ in range(2, RUNS):
                anchors.append(
                    tuple(
                        tuple(twice * b - a for a, b in zip(old, new))
                        for old, new in zip(anchors[-2], anchors[-1])
                    )
                )
            twice = 2.0 * turn[0]
            for r, (first, second) in enumerate(anchors):
                for part, ref in enumerate((right_cos, right_sin)):
                    before, now = first[part], second[part]
                    for j in range(0, STEPS, 2):
                        if j:
                            before = twice * now - before
                            now = twice * before - now
                        put(ref, r * RUN_ROWS + j * 8, before, now)

    def multiply(slot):
        left_cos, left_sin, right_cos, right_sin = slot
        contract = (((1,), (1,)), ((), ()))
        for i, (left, right) in enumerate(((left_cos, right_cos), (left_sin, right_sin))):
            acc[i] += lax.dot_general(
                left[...], right[...], contract, preferred_element_type=jnp.float32
            )

    slot_a, slot_b = slots[:4], slots[4:]
    acc[...] = jnp.zeros_like(acc)
    generate(0, slot_a)

    def step(i, carry):
        first = i * (2 * CHUNK_BLOCKS)
        generate(first + CHUNK_BLOCKS, slot_b)
        multiply(slot_a)
        generate(lax.rem(first + 2 * CHUNK_BLOCKS, BLOCKS), slot_a)
        multiply(slot_b)
        return carry

    lax.fori_loop(0, CHUNKS // 2, step, 0)
    for f in range(FACETS):
        for r in range(RUNS):
            at = (f * RUNS + r) * RUN_HALF
            for i in range(2):
                column = (f * 2 + i) * HALF
                for k in range(RUN_HALF // OUT_ROWS):
                    rows = slice(at + k * OUT_ROWS, at + (k + 1) * OUT_ROWS)
                    rows_imag = slice(at + HALF + k * OUT_ROWS, at + HALF + (k + 1) * OUT_ROWS)
                    a, b = acc[i, rows], acc[i, rows_imag]
                    below, above = (a - b, a + b) if i == 0 else (b + a, b - a)
                    for place, values in ((2 + k, below), (1 - k, above)):
                        out_ref[r * 4 + place, :, column : column + HALF] = values.astype(jnp.bfloat16)


def combine_kernel(scale, place_ref, data_ref, out_ref):
    shape = (OUT_ROWS, PEERS * OUT_ROWS)
    out_row = lax.broadcasted_iota(jnp.int32, shape, 0)
    sent_row = lax.broadcasted_iota(jnp.int32, shape, 1) % OUT_ROWS
    wanted = jnp.where(place_ref[0] < 2, OUT_ROWS - 1 - out_row, out_row)
    pick = (sent_row == wanted).astype(jnp.bfloat16)
    total = jnp.dot(pick, data_ref[...].reshape(PEERS * OUT_ROWS, FACETS * PIX), preferred_element_type=jnp.float32) * scale
    flip = (
        lax.broadcasted_iota(jnp.int32, (HALF, HALF), 0)
        + lax.broadcasted_iota(jnp.int32, (HALF, HALF), 1)
        == HALF - 1
    ).astype(jnp.bfloat16)
    evens = [total[:, f * PIX : f * PIX + HALF] for f in range(FACETS)]
    odds = [total[:, f * PIX + HALF : (f + 1) * PIX] for f in range(FACETS)]
    rest = jnp.concatenate([even + odd for even, odd in zip(evens, odds)], axis=0)
    pieces = []
    for _ in range(3):
        pieces.append(rest.astype(jnp.bfloat16))
        rest = rest - pieces[-1].astype(jnp.float32)
    turned = jnp.dot(jnp.concatenate(pieces, axis=0), flip, preferred_element_type=jnp.float32)
    rows = FACETS * OUT_ROWS
    mirrored = turned[:rows] + turned[rows : 2 * rows] + turned[2 * rows :]
    for f in range(FACETS):
        out_ref[0, :, f * PIX : f * PIX + HALF] = mirrored[f * OUT_ROWS : (f + 1) * OUT_ROWS]
        out_ref[0, :, f * PIX + HALF : (f + 1) * PIX] = evens[f] - odds[f]


VMEM = pl.BlockSpec(memory_space=pltpu.VMEM)
SMEM = pl.BlockSpec(memory_space=pltpu.SMEM)


def pack(visibility, weights, positions, station_pairs):
    return pl.pallas_call(
        pack_kernel,
        out_shape=jax.ShapeDtypeStruct((SOURCES, 4 * READ_ROWS, LANES), jnp.float32),
        in_specs=[VMEM, VMEM, SMEM, SMEM],
        out_specs=VMEM,
        name="pack",
    )(visibility, weights, positions, station_pairs)


def make_images(half, facet_shift, arrived):
    slot = [
        pltpu.VMEM((FACETS * HALF, CHUNK), jnp.bfloat16),
        pltpu.VMEM((FACETS * HALF, CHUNK), jnp.bfloat16),
        pltpu.VMEM((HALF, CHUNK), jnp.bfloat16),
        pltpu.VMEM((HALF, CHUNK), jnp.bfloat16),
    ]
    return pl.pallas_call(
        image_kernel,
        out_shape=jax.ShapeDtypeStruct((PEERS, OUT_ROWS, FACETS * PIX), jnp.bfloat16),
        in_specs=[SMEM, SMEM, VMEM],
        out_specs=VMEM,
        scratch_shapes=[
            pltpu.VMEM((TABLE, BLOCKS, LANES), jnp.float32),
            pltpu.VMEM((2, FACETS * HALF, HALF), jnp.float32),
            *slot,
            *slot,
        ],
        compiler_params=pltpu.CompilerParams(vmem_limit_bytes=40 * 1024 * 1024),
        name="images",
    )(half, facet_shift, arrived)


def combine(scale, place, parts):
    return pl.pallas_call(
        functools.partial(combine_kernel, scale),
        out_shape=jax.ShapeDtypeStruct((1, OUT_ROWS, FACETS * PIX), jnp.float32),
        in_specs=[SMEM, VMEM],
        out_specs=VMEM,
        compiler_params=pltpu.CompilerParams(vmem_limit_bytes=8 * 1024 * 1024),
        name="combine",
    )(place, parts)


def body(visibility, weights, positions, station_pairs, facet_shift):
    half = lax.axis_index("zh").astype(jnp.int32).reshape(1)
    place = lax.axis_index("x").astype(jnp.int32).reshape(1)
    packed = pack(visibility, weights, positions, station_pairs)
    arrived = lax.all_to_all(packed, ("chan", "zh"), split_axis=0, concat_axis=0, tiled=True)
    images = make_images(half, facet_shift, arrived)
    parts = lax.all_to_all(
        images, ("y", "x"), split_axis=0, concat_axis=0, tiled=True
    )
    scale = 1.0 / math.sqrt(READ_ROWS * GROUPS * 32 * LANES)
    return combine(scale, place, parts)


def solution(mesh):
    fine = Mesh(mesh.devices.reshape(GROUPS, 4, HALVES, 4), ("chan", "y", "zh", "x"))
    line = ("y", "zh", "x")
    in_specs = (
        P(None, ("chan", *line), None),
        P(("chan", *line), None),
        P(),
        P(None, ("chan", *line)),
        P(),
    )
    out_specs = P("chan", line, None)
    return jax.shard_map(body, mesh=fine, in_specs=in_specs, out_specs=out_specs, check_vma=False)
```

```python
import functools
import math

import jax
import jax.numpy as jnp
from jax import lax
from jax.experimental import pallas as pl
from jax.experimental.pallas import tpu as pltpu
from jax.sharding import Mesh, PartitionSpec as P

PIX = 512
HALF = PIX // 2
FACETS = 2
CHANNELS = 1024
GROUPS = 8
LANES = 128
READ_ROWS = 4
RUN_ROWS = 64
RUNS = 4
STEPS = RUN_ROWS // 8
RUN_HALF = RUN_ROWS // 2
HALVES = 2
BLOCKS = GROUPS * READ_ROWS
CHUNK_BLOCKS = 4
CHUNK = CHUNK_BLOCKS * LANES
CHUNKS = BLOCKS // CHUNK_BLOCKS
PEERS = 16
OUT_ROWS = 16
COS_COEF = (
    1.0, -19.739208221435547, 64.93939208984375, -85.45665740966797,
    60.242130279541016, -26.4046688079834, 7.800131797790527, -1.4531123638153076,
)
SIN_COEF = (
    6.2831854820251465, -41.34170150756836, 81.60513305664062, -76.70301818847656,
    42.02592849731445, -14.899847984313965, 3.238137722015381,
)


def poly(coef, z):
    total = jnp.full_like(z, coef[-1])
    for c in coef[-2::-1]:
        total = total * z + c
    return total


def frac(turns):
    return turns - jnp.floor(turns + 0.5)


def cos_sin_reduced(r):
    z = r * r
    return poly(COS_COEF, z), poly(SIN_COEF, z) * r


def cos_sin(turns):
    return cos_sin_reduced(frac(turns))


def pack_kernel(vis_ref, weight_ref, pos_ref, pair_ref, out_ref):
    weight = weight_ref[...].astype(jnp.float32)
    real = weight * vis_ref[0].astype(jnp.float32)
    imag = weight * vis_ref[1].astype(jnp.float32)
    shape = (READ_ROWS, CHANNELS)
    channel = lax.broadcasted_iota(jnp.int32, shape, 1).astype(jnp.float32)
    frequency = 1.0 + channel / CHANNELS
    row = lax.broadcasted_iota(jnp.int32, shape, 0)
    spans = []
    for axis in range(2):
        span = jnp.zeros(shape, jnp.float32)
        for b in range(READ_ROWS):
            value = pos_ref[axis, pair_ref[0, b]] - pos_ref[axis, pair_ref[1, b]]
            span = jnp.where(row == b, value, span)
        spans.append(span * frequency)
    for a, values in enumerate((real, imag, *spans)):
        for g in range(GROUPS):
            part = values[:, g * LANES : (g + 1) * LANES]
            out_ref[g, a * READ_ROWS : (a + 1) * READ_ROWS, :] = part


PHASED = 0
EAST, NORTH, C8E, S8E, C8N, S8N, C64N, S64N, TABLE = range(2 * FACETS * RUNS, 2 * FACETS * RUNS + 9)


def rotate(u, turn):
    (ur, ui), (c, s) = u, turn
    return ur * c - ui * s, ur * s + ui * c


def first_kernel(half_ref, shift_ref, data_ref, acc, table, *slots):
    add_rows(half_ref, shift_ref, data_ref, table, acc, slots)


def last_kernel(
    half_ref, shift_ref, data_ref, earlier_ref, out_ref, table, acc, earlier, arrived, *slots
):
    copy = pltpu.make_async_copy(earlier_ref, earlier, arrived)
    copy.start()
    add_rows(half_ref, shift_ref, data_ref, table, acc, slots)
    copy.wait()
    for f in range(FACETS):
        for r in range(RUNS):
            at = (f * RUNS + r) * RUN_HALF
            for i in range(2):
                column = (f * 2 + i) * HALF
                for k in range(RUN_HALF // OUT_ROWS):
                    rows = slice(at + k * OUT_ROWS, at + (k + 1) * OUT_ROWS)
                    rows_imag = slice(at + HALF + k * OUT_ROWS, at + HALF + (k + 1) * OUT_ROWS)
                    a = acc[i, rows] + earlier[i, rows]
                    b = acc[i, rows_imag] + earlier[i, rows_imag]
                    below, above = (a - b, a + b) if i == 0 else (b + a, b - a)
                    for place, values in ((2 + k, below), (1 - k, above)):
                        out_ref[r * 4 + place, :, column : column + HALF] = values.astype(jnp.bfloat16)


def add_rows(half_ref, shift_ref, data_ref, table, acc, slots):
    for s in range(GROUPS):
        for a, t in enumerate((PHASED, PHASED + 1, EAST, NORTH)):
            table[t, s * READ_ROWS : (s + 1) * READ_ROWS, :] = data_ref[
                s, a * READ_ROWS : (a + 1) * READ_ROWS, :
            ]
    base_row = (half_ref[0] * RUN_ROWS - HALF).astype(jnp.float32) + (RUN_HALF - 0.5)

    def prepare(i, carry):
        rows = pl.ds(pl.multiple_of(i * 8, 8), 8)
        east = table[EAST, rows, :]
        north = table[NORTH, rows, :]
        seen = table[PHASED, rows, :], table[PHASED + 1, rows, :]
        next_run = cos_sin(east * (2.0 * RUN_ROWS / PIX))
        for f in range(FACETS):
            left = (shift_ref[0, f].astype(jnp.float32) + base_row) * (1.0 / PIX)
            right = (shift_ref[1, f].astype(jnp.float32) - 0.5) * (1.0 / PIX)
            phased = rotate(seen, cos_sin(frac(east * left) + frac(north * right)))
            for r in range(RUNS):
                if r:
                    phased = rotate(phased, next_run)
                at = PHASED + 2 * (f * RUNS + r)
                table[at, rows, :], table[at + 1, rows, :] = phased
        for t, turns in (
            (C8E, east * (8.0 / PIX)),
            (C8N, north * (8.0 / PIX)),
            (C64N, north * (64.0 / PIX)),
        ):
            cos, sin = cos_sin(turns)
            table[t, rows, :] = cos
            table[t + 1, rows, :] = sin
        return carry

    lax.fori_loop(0, BLOCKS // 8, prepare, 0, unroll=4)

    offsets = lax.broadcasted_iota(jnp.int32, (8, LANES), 0).astype(jnp.float32) + 0.5
    offsets = offsets * (1.0 / PIX)

    def generate(first_block, slot):
        left_cos, left_sin, right_cos, right_sin = slot
        for t in range(CHUNK_BLOCKS):
            block = first_block + t
            lanes = slice(t * LANES, (t + 1) * LANES)

            def row(i):
                return jnp.broadcast_to(table[i, pl.ds(block, 1), :], (8, LANES))

            def put(ref, at, first, second):
                ref[at : at + 16, lanes] = jnp.concatenate([first, second], axis=0).astype(
                    jnp.bfloat16
                )

            base = cos_sin(row(EAST) * offsets)
            turn = (row(C8E), row(S8E))
            wave = [base, rotate(base, turn)]
            twice = 2.0 * turn[0]
            for _ in range(2, RUN_HALF // 8):
                wave.append(tuple(twice * b - a for a, b in zip(wave[-2], wave[-1])))
            for f in range(FACETS):
                for r in range(RUNS):
                    index = PHASED + 2 * (f * RUNS + r)
                    real, imag = row(index), row(index + 1)
                    at = (f * RUNS + r) * RUN_HALF
                    for j in range(0, RUN_HALF // 8, 2):
                        (c0, s0), (c1, s1) = wave[j], wave[j + 1]
                        put(left_cos, at + j * 8, real * c0, real * c1)
                        put(left_cos, at + HALF + j * 8, imag * s0, imag * s1)
                        put(left_sin, at + j * 8, real * s0, real * s1)
                        put(left_sin, at + HALF + j * 8, imag * c0, imag * c1)

            start = cos_sin(row(NORTH) * offsets)
            turn = (row(C8N), row(S8N))
            next_run = (row(C64N), row(S64N))
            anchors = [(start, rotate(start, turn))]
            anchors.append(tuple(rotate(u, next_run) for u in anchors[0]))
            twice = 2.0 * next_run[0]
            for _ in range(2, RUNS):
                anchors.append(
                    tuple(
                        tuple(twice * b - a for a, b in zip(old, new))
                        for old, new in zip(anchors[-2], anchors[-1])
                    )
                )
            twice = 2.0 * turn[0]
            for r, (first, second) in enumerate(anchors):
                for part, ref in enumerate((right_cos, right_sin)):
                    before, now = first[part], second[part]
                    for j in range(0, STEPS, 2):
                        if j:
                            before = twice * now - before
                            now = twice * before - now
                        put(ref, r * RUN_ROWS + j * 8, before, now)

    def multiply(slot):
        left_cos, left_sin, right_cos, right_sin = slot
        contract = (((1,), (1,)), ((), ()))
        for i, (left, right) in enumerate(((left_cos, right_cos), (left_sin, right_sin))):
            acc[i] += lax.dot_general(
                left[...], right[...], contract, preferred_element_type=jnp.float32
            )

    slot_a, slot_b = slots[:4], slots[4:]
    acc[...] = jnp.zeros_like(acc)
    generate(0, slot_a)

    def step(i, carry):
        first = i * (2 * CHUNK_BLOCKS)
        generate(first + CHUNK_BLOCKS, slot_b)
        multiply(slot_a)
        generate(lax.rem(first + 2 * CHUNK_BLOCKS, BLOCKS), slot_a)
        multiply(slot_b)
        return carry

    lax.fori_loop(0, CHUNKS // 2, step, 0)


def combine_kernel(scale, place_ref, data_ref, out_ref):
    shape = (OUT_ROWS, PEERS * OUT_ROWS)
    out_row = lax.broadcasted_iota(jnp.int32, shape, 0)
    sent_row = lax.broadcasted_iota(jnp.int32, shape, 1) % OUT_ROWS
    wanted = jnp.where(place_ref[0] < 2, OUT_ROWS - 1 - out_row, out_row)
    pick = (sent_row == wanted).astype(jnp.bfloat16)
    total = jnp.dot(pick, data_ref[...].reshape(PEERS * OUT_ROWS, FACETS * PIX), preferred_element_type=jnp.float32) * scale
    flip = (
        lax.broadcasted_iota(jnp.int32, (HALF, HALF), 0)
        + lax.broadcasted_iota(jnp.int32, (HALF, HALF), 1)
        == HALF - 1
    ).astype(jnp.bfloat16)
    evens = [total[:, f * PIX : f * PIX + HALF] for f in range(FACETS)]
    odds = [total[:, f * PIX + HALF : (f + 1) * PIX] for f in range(FACETS)]
    rest = jnp.concatenate([even + odd for even, odd in zip(evens, odds)], axis=0)
    pieces = []
    for _ in range(3):
        pieces.append(rest.astype(jnp.bfloat16))
        rest = rest - pieces[-1].astype(jnp.float32)
    turned = jnp.dot(jnp.concatenate(pieces, axis=0), flip, preferred_element_type=jnp.float32)
    rows = FACETS * OUT_ROWS
    mirrored = turned[:rows] + turned[rows : 2 * rows] + turned[2 * rows :]
    for f in range(FACETS):
        out_ref[0, :, f * PIX : f * PIX + HALF] = mirrored[f * OUT_ROWS : (f + 1) * OUT_ROWS]
        out_ref[0, :, f * PIX + HALF : (f + 1) * PIX] = evens[f] - odds[f]


VMEM = pl.BlockSpec(memory_space=pltpu.VMEM)
SMEM = pl.BlockSpec(memory_space=pltpu.SMEM)


def pack(visibility, weights, positions, station_pairs):
    return pl.pallas_call(
        pack_kernel,
        out_shape=jax.ShapeDtypeStruct((GROUPS, 4 * READ_ROWS, LANES), jnp.float32),
        in_specs=[VMEM, VMEM, SMEM, SMEM],
        out_specs=VMEM,
        name="pack",
    )(visibility, weights, positions, station_pairs)


SUMS = (2, FACETS * HALF, HALF)
ROWS_COST = pl.CostEstimate(
    flops=2 * math.prod(SUMS) * BLOCKS * LANES, bytes_accessed=4 * math.prod(SUMS), transcendentals=0
)
TABLE_SCRATCH = pltpu.VMEM((TABLE, BLOCKS, LANES), jnp.float32)
SLOT = [
    pltpu.VMEM((FACETS * HALF, CHUNK), jnp.bfloat16),
    pltpu.VMEM((FACETS * HALF, CHUNK), jnp.bfloat16),
    pltpu.VMEM((HALF, CHUNK), jnp.bfloat16),
    pltpu.VMEM((HALF, CHUNK), jnp.bfloat16),
]
IMAGE_PARAMS = pltpu.CompilerParams(vmem_limit_bytes=24 * 1024 * 1024)


def first_sums(half, facet_shift, arrived):
    return pl.pallas_call(
        first_kernel,
        out_shape=jax.ShapeDtypeStruct(SUMS, jnp.float32),
        in_specs=[SMEM, SMEM, VMEM],
        out_specs=VMEM,
        scratch_shapes=[TABLE_SCRATCH, *SLOT, *SLOT],
        compiler_params=IMAGE_PARAMS,
        cost_estimate=ROWS_COST,
        name="first_sums",
    )(half, facet_shift, arrived)


def make_images(half, facet_shift, arrived, earlier):
    return pl.pallas_call(
        last_kernel,
        out_shape=jax.ShapeDtypeStruct((PEERS, OUT_ROWS, FACETS * PIX), jnp.bfloat16),
        in_specs=[SMEM, SMEM, VMEM, pl.BlockSpec(memory_space=pl.ANY)],
        out_specs=VMEM,
        scratch_shapes=[
            TABLE_SCRATCH,
            pltpu.VMEM(SUMS, jnp.float32),
            pltpu.VMEM(SUMS, jnp.float32),
            pltpu.SemaphoreType.DMA,
            *SLOT,
            *SLOT,
        ],
        compiler_params=IMAGE_PARAMS,
        cost_estimate=ROWS_COST,
        name="images",
    )(half, facet_shift, arrived, earlier)


def combine(scale, place, parts):
    return pl.pallas_call(
        functools.partial(combine_kernel, scale),
        out_shape=jax.ShapeDtypeStruct((1, OUT_ROWS, FACETS * PIX), jnp.float32),
        in_specs=[SMEM, VMEM],
        out_specs=VMEM,
        compiler_params=pltpu.CompilerParams(vmem_limit_bytes=8 * 1024 * 1024),
        name="combine",
    )(place, parts)


def body(visibility, weights, positions, station_pairs, facet_shift):
    half = lax.axis_index("zh").astype(jnp.int32).reshape(1)
    place = lax.axis_index("x").astype(jnp.int32).reshape(1)
    packed = pack(visibility, weights, positions, station_pairs)
    own = lax.all_to_all(packed, "chan", split_axis=0, concat_axis=0, tiled=True)
    other = lax.ppermute(own, "zh", [(h, HALVES - 1 - h) for h in range(HALVES)])
    earlier = first_sums(half, facet_shift, own)
    images = make_images(half, facet_shift, other, earlier)
    parts = lax.all_to_all(
        images, ("y", "x"), split_axis=0, concat_axis=0, tiled=True
    )
    scale = 1.0 / math.sqrt(READ_ROWS * GROUPS * 32 * LANES)
    return combine(scale, place, parts)


def solution(mesh):
    fine = Mesh(mesh.devices.reshape(GROUPS, 4, HALVES, 4), ("chan", "y", "zh", "x"))
    line = ("y", "zh", "x")
    in_specs = (
        P(None, ("chan", *line), None),
        P(("chan", *line), None),
        P(),
        P(None, ("chan", *line)),
        P(),
    )
    out_specs = P("chan", line, None)
    return jax.shard_map(body, mesh=fine, in_specs=in_specs, out_specs=out_specs, check_vma=False)
```

```python
import functools
import math

import jax
import jax.numpy as jnp
from jax import lax
from jax.experimental import pallas as pl
from jax.experimental.pallas import tpu as pltpu
from jax.sharding import Mesh, PartitionSpec as P

PIX = 512
HALF = PIX // 2
FACETS = 2
CHANNELS = 1024
GROUPS = 8
LANES = 128
READ_ROWS = 4
RUN_ROWS = 64
RUNS = 4
STEPS = RUN_ROWS // 8
RUN_HALF = RUN_ROWS // 2
HALVES = 2
BLOCKS = GROUPS * READ_ROWS
PEERS = 16
OUT_ROWS = 16
COS_COEF = (
    1.0, -19.739208221435547, 64.93939208984375, -85.45665740966797,
    60.242130279541016, -26.4046688079834, 7.800131797790527, -1.4531123638153076,
)
SIN_COEF = (
    6.2831854820251465, -41.34170150756836, 81.60513305664062, -76.70301818847656,
    42.02592849731445, -14.899847984313965, 3.238137722015381,
)


def poly(coef, z):
    total = jnp.full_like(z, coef[-1])
    for c in coef[-2::-1]:
        total = total * z + c
    return total


def frac(turns):
    return turns - jnp.floor(turns + 0.5)


def cos_sin_reduced(r):
    z = r * r
    return poly(COS_COEF, z), poly(SIN_COEF, z) * r


def cos_sin(turns):
    return cos_sin_reduced(frac(turns))


def pack_kernel(vis_ref, weight_ref, pos_ref, pair_ref, out_ref):
    weight = weight_ref[...].astype(jnp.float32)
    real = weight * vis_ref[0].astype(jnp.float32)
    imag = weight * vis_ref[1].astype(jnp.float32)
    shape = (READ_ROWS, CHANNELS)
    channel = lax.broadcasted_iota(jnp.int32, shape, 1).astype(jnp.float32)
    frequency = 1.0 + channel / CHANNELS
    row = lax.broadcasted_iota(jnp.int32, shape, 0)
    spans = []
    for axis in range(2):
        span = jnp.zeros(shape, jnp.float32)
        for b in range(READ_ROWS):
            value = pos_ref[axis, pair_ref[0, b]] - pos_ref[axis, pair_ref[1, b]]
            span = jnp.where(row == b, value, span)
        spans.append(span * frequency)
    for a, values in enumerate((real, imag, *spans)):
        for g in range(GROUPS):
            part = values[:, g * LANES : (g + 1) * LANES]
            out_ref[g, a * READ_ROWS : (a + 1) * READ_ROWS, :] = part


PHASED = 0
EAST, NORTH, C8E, S8E, C8N, S8N, C64N, S64N, TABLE = range(2 * FACETS * RUNS, 2 * FACETS * RUNS + 9)


def rotate(u, turn):
    (ur, ui), (c, s) = u, turn
    return ur * c - ui * s, ur * s + ui * c


def first_kernel(half_ref, shift_ref, data_ref, out_ref, table, *panels):
    for i, sums in enumerate(image_sums(half_ref, shift_ref, data_ref, table, panels)):
        out_ref[i] = sums


def last_kernel(
    half_ref, shift_ref, data_ref, earlier_ref, out_ref, table, acc, *panels
):
    for i, sums in enumerate(image_sums(half_ref, shift_ref, data_ref, table, panels)):
        acc[i] = sums + earlier_ref[i]
    for f in range(FACETS):
        for r in range(RUNS):
            at = (f * RUNS + r) * RUN_HALF
            for i in range(2):
                column = (f * 2 + i) * HALF
                for k in range(RUN_HALF // OUT_ROWS):
                    rows = slice(at + k * OUT_ROWS, at + (k + 1) * OUT_ROWS)
                    rows_imag = slice(at + HALF + k * OUT_ROWS, at + HALF + (k + 1) * OUT_ROWS)
                    a, b = acc[i, rows], acc[i, rows_imag]
                    below, above = (a - b, a + b) if i == 0 else (b + a, b - a)
                    for place, values in ((2 + k, below), (1 - k, above)):
                        out_ref[r * 4 + place, :, column : column + HALF] = values.astype(jnp.bfloat16)


def image_sums(half_ref, shift_ref, data_ref, table, panels):
    for s in range(GROUPS):
        for a, t in enumerate((PHASED, PHASED + 1, EAST, NORTH)):
            table[t, s * READ_ROWS : (s + 1) * READ_ROWS, :] = data_ref[
                s, a * READ_ROWS : (a + 1) * READ_ROWS, :
            ]
    base_row = (half_ref[0] * RUN_ROWS - HALF).astype(jnp.float32) + (RUN_HALF - 0.5)

    for i in range(BLOCKS // 8):
        rows = slice(i * 8, (i + 1) * 8)
        east = table[EAST, rows, :]
        north = table[NORTH, rows, :]
        seen = table[PHASED, rows, :], table[PHASED + 1, rows, :]
        next_run = cos_sin(east * (2.0 * RUN_ROWS / PIX))
        for f in range(FACETS):
            left = (shift_ref[0, f].astype(jnp.float32) + base_row) * (1.0 / PIX)
            right = (shift_ref[1, f].astype(jnp.float32) - 0.5) * (1.0 / PIX)
            phased = rotate(seen, cos_sin(frac(east * left) + frac(north * right)))
            for r in range(RUNS):
                if r:
                    phased = rotate(phased, next_run)
                at = PHASED + 2 * (f * RUNS + r)
                table[at, rows, :], table[at + 1, rows, :] = phased
        for t, turns in (
            (C8E, east * (8.0 / PIX)),
            (C8N, north * (8.0 / PIX)),
            (C64N, north * (64.0 / PIX)),
        ):
            cos, sin = cos_sin(turns)
            table[t, rows, :] = cos
            table[t + 1, rows, :] = sin

    offsets = lax.broadcasted_iota(jnp.int32, (8, LANES), 0).astype(jnp.float32) + 0.5
    offsets = offsets * (1.0 / PIX)

    panels = [panels[i : i + 4] for i in range(0, len(panels), 4)]
    for block, (left_cos, left_sin, right_cos, right_sin) in enumerate(panels):

        def row(i):
            return jnp.broadcast_to(table[i, block : block + 1, :], (8, LANES))

        def put(ref, at, first, second):
            ref[at : at + 16, :] = jnp.concatenate([first, second], axis=0).astype(jnp.bfloat16)

        base = cos_sin(row(EAST) * offsets)
        turn = (row(C8E), row(S8E))
        wave = [base, rotate(base, turn)]
        twice = 2.0 * turn[0]
        for _ in range(2, RUN_HALF // 8):
            wave.append(tuple(twice * b - a for a, b in zip(wave[-2], wave[-1])))
        for f in range(FACETS):
            for r in range(RUNS):
                index = PHASED + 2 * (f * RUNS + r)
                real, imag = row(index), row(index + 1)
                at = (f * RUNS + r) * RUN_HALF
                for j in range(0, RUN_HALF // 8, 2):
                    (c0, s0), (c1, s1) = wave[j], wave[j + 1]
                    put(left_cos, at + j * 8, real * c0, real * c1)
                    put(left_cos, at + HALF + j * 8, imag * s0, imag * s1)
                    put(left_sin, at + j * 8, real * s0, real * s1)
                    put(left_sin, at + HALF + j * 8, imag * c0, imag * c1)

        start = cos_sin(row(NORTH) * offsets)
        turn = (row(C8N), row(S8N))
        next_run = (row(C64N), row(S64N))
        anchors = [(start, rotate(start, turn))]
        anchors.append(tuple(rotate(u, next_run) for u in anchors[0]))
        twice = 2.0 * next_run[0]
        for _ in range(2, RUNS):
            anchors.append(
                tuple(
                    tuple(twice * b - a for a, b in zip(old, new))
                    for old, new in zip(anchors[-2], anchors[-1])
                )
            )
        twice = 2.0 * turn[0]
        for r, (first, second) in enumerate(anchors):
            for part, ref in enumerate((right_cos, right_sin)):
                before, now = first[part], second[part]
                for j in range(0, STEPS, 2):
                    if j:
                        before = twice * now - before
                        now = twice * before - now
                    put(ref, r * RUN_ROWS + j * 8, before, now)

    left_cos, left_sin, right_cos, right_sin = (
        jnp.concatenate([ref[...] for ref in refs], axis=1) for refs in zip(*panels)
    )
    contract = (((1,), (1,)), ((), ()))
    for left, right in ((left_cos, right_cos), (left_sin, right_sin)):
        yield lax.dot_general(left, right, contract, preferred_element_type=jnp.float32)


def combine_kernel(scale, place_ref, data_ref, out_ref):
    shape = (OUT_ROWS, PEERS * OUT_ROWS)
    out_row = lax.broadcasted_iota(jnp.int32, shape, 0)
    sent_row = lax.broadcasted_iota(jnp.int32, shape, 1) % OUT_ROWS
    wanted = jnp.where(place_ref[0] < 2, OUT_ROWS - 1 - out_row, out_row)
    pick = (sent_row == wanted).astype(jnp.bfloat16)
    total = jnp.dot(pick, data_ref[...].reshape(PEERS * OUT_ROWS, FACETS * PIX), preferred_element_type=jnp.float32) * scale
    flip = (
        lax.broadcasted_iota(jnp.int32, (HALF, HALF), 0)
        + lax.broadcasted_iota(jnp.int32, (HALF, HALF), 1)
        == HALF - 1
    ).astype(jnp.bfloat16)
    evens = [total[:, f * PIX : f * PIX + HALF] for f in range(FACETS)]
    odds = [total[:, f * PIX + HALF : (f + 1) * PIX] for f in range(FACETS)]
    rest = jnp.concatenate([even + odd for even, odd in zip(evens, odds)], axis=0)
    pieces = []
    for _ in range(3):
        pieces.append(rest.astype(jnp.bfloat16))
        rest = rest - pieces[-1].astype(jnp.float32)
    turned = jnp.dot(jnp.concatenate(pieces, axis=0), flip, preferred_element_type=jnp.float32)
    rows = FACETS * OUT_ROWS
    mirrored = turned[:rows] + turned[rows : 2 * rows] + turned[2 * rows :]
    for f in range(FACETS):
        out_ref[0, :, f * PIX : f * PIX + HALF] = mirrored[f * OUT_ROWS : (f + 1) * OUT_ROWS]
        out_ref[0, :, f * PIX + HALF : (f + 1) * PIX] = evens[f] - odds[f]


VMEM = pl.BlockSpec(memory_space=pltpu.VMEM)
SMEM = pl.BlockSpec(memory_space=pltpu.SMEM)


def pack(visibility, weights, positions, station_pairs):
    return pl.pallas_call(
        pack_kernel,
        out_shape=jax.ShapeDtypeStruct((GROUPS, 4 * READ_ROWS, LANES), jnp.float32),
        in_specs=[VMEM, VMEM, SMEM, SMEM],
        out_specs=VMEM,
        name="pack",
    )(visibility, weights, positions, station_pairs)


SUMS = (2, FACETS * HALF, HALF)
ROWS_COST = pl.CostEstimate(
    flops=2 * math.prod(SUMS) * BLOCKS * LANES, bytes_accessed=4 * math.prod(SUMS), transcendentals=0
)
TABLE_SCRATCH = pltpu.VMEM((TABLE, BLOCKS, LANES), jnp.float32)
PANELS = [
    pltpu.VMEM((FACETS * HALF, LANES), jnp.bfloat16),
    pltpu.VMEM((FACETS * HALF, LANES), jnp.bfloat16),
    pltpu.VMEM((HALF, LANES), jnp.bfloat16),
    pltpu.VMEM((HALF, LANES), jnp.bfloat16),
] * BLOCKS
IMAGE_PARAMS = pltpu.CompilerParams(vmem_limit_bytes=32 * 1024 * 1024)


def first_sums(half, facet_shift, arrived):
    return pl.pallas_call(
        first_kernel,
        out_shape=jax.ShapeDtypeStruct(SUMS, jnp.float32),
        in_specs=[SMEM, SMEM, VMEM],
        out_specs=VMEM,
        scratch_shapes=[TABLE_SCRATCH, *PANELS],
        compiler_params=IMAGE_PARAMS,
        cost_estimate=ROWS_COST,
        name="first_sums",
    )(half, facet_shift, arrived)


def make_images(half, facet_shift, arrived, earlier):
    return pl.pallas_call(
        last_kernel,
        out_shape=jax.ShapeDtypeStruct((PEERS, OUT_ROWS, FACETS * PIX), jnp.bfloat16),
        in_specs=[SMEM, SMEM, VMEM, VMEM],
        out_specs=VMEM,
        scratch_shapes=[
            TABLE_SCRATCH,
            pltpu.VMEM(SUMS, jnp.float32),
            *PANELS,
        ],
        compiler_params=IMAGE_PARAMS,
        cost_estimate=ROWS_COST,
        name="images",
    )(half, facet_shift, arrived, earlier)


def combine(scale, place, parts):
    return pl.pallas_call(
        functools.partial(combine_kernel, scale),
        out_shape=jax.ShapeDtypeStruct((1, OUT_ROWS, FACETS * PIX), jnp.float32),
        in_specs=[SMEM, VMEM],
        out_specs=VMEM,
        compiler_params=pltpu.CompilerParams(vmem_limit_bytes=8 * 1024 * 1024),
        name="combine",
    )(place, parts)


def body(visibility, weights, positions, station_pairs, facet_shift):
    half = lax.axis_index("zh").astype(jnp.int32).reshape(1)
    place = lax.axis_index("x").astype(jnp.int32).reshape(1)
    packed = pack(visibility, weights, positions, station_pairs)
    own = lax.all_to_all(packed, "chan", split_axis=0, concat_axis=0, tiled=True)
    other = lax.ppermute(own, "zh", [(h, HALVES - 1 - h) for h in range(HALVES)])
    earlier = first_sums(half, facet_shift, own)
    images = make_images(half, facet_shift, other, earlier)
    parts = lax.all_to_all(
        images, ("y", "x"), split_axis=0, concat_axis=0, tiled=True
    )
    scale = 1.0 / math.sqrt(READ_ROWS * GROUPS * 32 * LANES)
    return combine(scale, place, parts)


def solution(mesh):
    fine = Mesh(mesh.devices.reshape(GROUPS, 4, HALVES, 4), ("chan", "y", "zh", "x"))
    line = ("y", "zh", "x")
    in_specs = (
        P(None, ("chan", *line), None),
        P(("chan", *line), None),
        P(),
        P(None, ("chan", *line)),
        P(),
    )
    out_specs = P("chan", line, None)
    return jax.shard_map(body, mesh=fine, in_specs=in_specs, out_specs=out_specs, check_vma=False)
```

```python
import functools
import math

import jax
import jax.numpy as jnp
from jax import lax
from jax.experimental import pallas as pl
from jax.experimental.pallas import tpu as pltpu
from jax.sharding import Mesh, PartitionSpec as P

PIX = 512
HALF = PIX // 2
FACETS = 2
CHANNELS = 1024
GROUPS = 8
LANES = 128
READ_ROWS = 4
RUN_ROWS = 64
RUNS = 4
STEPS = RUN_ROWS // 8
RUN_HALF = RUN_ROWS // 2
HALVES = 2
BLOCKS = GROUPS * READ_ROWS
PEERS = 16
OUT_ROWS = 16
COS_COEF = (
    1.0, -19.739208221435547, 64.93939208984375, -85.45665740966797,
    60.242130279541016, -26.4046688079834, 7.800131797790527, -1.4531123638153076,
)
SIN_COEF = (
    6.2831854820251465, -41.34170150756836, 81.60513305664062, -76.70301818847656,
    42.02592849731445, -14.899847984313965, 3.238137722015381,
)


def poly(coef, z):
    total = jnp.full_like(z, coef[-1])
    for c in coef[-2::-1]:
        total = total * z + c
    return total


def frac(turns):
    return turns - jnp.floor(turns + 0.5)


def cos_sin_reduced(r):
    z = r * r
    return poly(COS_COEF, z), poly(SIN_COEF, z) * r


def cos_sin(turns):
    return cos_sin_reduced(frac(turns))


def pack_kernel(vis_ref, weight_ref, pos_ref, pair_ref, out_ref):
    weight = weight_ref[...].astype(jnp.float32)
    real = weight * vis_ref[0].astype(jnp.float32)
    imag = weight * vis_ref[1].astype(jnp.float32)
    shape = (READ_ROWS, CHANNELS)
    channel = lax.broadcasted_iota(jnp.int32, shape, 1).astype(jnp.float32)
    frequency = 1.0 + channel / CHANNELS
    row = lax.broadcasted_iota(jnp.int32, shape, 0)
    spans = []
    for axis in range(2):
        span = jnp.zeros(shape, jnp.float32)
        for b in range(READ_ROWS):
            value = pos_ref[axis, pair_ref[0, b]] - pos_ref[axis, pair_ref[1, b]]
            span = jnp.where(row == b, value, span)
        spans.append(span * frequency)
    for a, values in enumerate((real, imag, *spans)):
        for g in range(GROUPS):
            part = values[:, g * LANES : (g + 1) * LANES]
            out_ref[g, a * READ_ROWS : (a + 1) * READ_ROWS, :] = part


PHASED = 0
EAST, NORTH, C8E, S8E, C8N, S8N, C64N, S64N, TABLE = range(2 * FACETS * RUNS, 2 * FACETS * RUNS + 9)


def rotate(u, turn):
    (ur, ui), (c, s) = u, turn
    return ur * c - ui * s, ur * s + ui * c


def first_kernel(half_ref, shift_ref, data_ref, out_ref, table, starts, *panels):
    for i, sums in enumerate(image_sums(half_ref, shift_ref, data_ref, table, starts, panels)):
        out_ref[i] = sums


def last_kernel(
    half_ref, shift_ref, data_ref, earlier_ref, out_ref, table, starts, acc, *panels
):
    for i, sums in enumerate(image_sums(half_ref, shift_ref, data_ref, table, starts, panels)):
        acc[i] = sums + earlier_ref[i]
    for f in range(FACETS):
        for r in range(RUNS):
            at = (f * RUNS + r) * RUN_HALF
            for i in range(2):
                column = (f * 2 + i) * HALF
                for k in range(RUN_HALF // OUT_ROWS):
                    rows = slice(at + k * OUT_ROWS, at + (k + 1) * OUT_ROWS)
                    rows_imag = slice(at + HALF + k * OUT_ROWS, at + HALF + (k + 1) * OUT_ROWS)
                    a, b = acc[i, rows], acc[i, rows_imag]
                    below, above = (a - b, a + b) if i == 0 else (b + a, b - a)
                    for place, values in ((2 + k, below), (1 - k, above)):
                        out_ref[r * 4 + place, :, column : column + HALF] = values.astype(jnp.bfloat16)


def image_sums(half_ref, shift_ref, data_ref, table, starts, panels):
    for s in range(GROUPS):
        for a, t in enumerate((PHASED, PHASED + 1, EAST, NORTH)):
            table[t, s * READ_ROWS : (s + 1) * READ_ROWS, :] = data_ref[
                s, a * READ_ROWS : (a + 1) * READ_ROWS, :
            ]
    base_row = (half_ref[0] * RUN_ROWS - HALF).astype(jnp.float32) + (RUN_HALF - 0.5)

    for i in range(BLOCKS // 8):
        rows = slice(i * 8, (i + 1) * 8)
        east = table[EAST, rows, :]
        north = table[NORTH, rows, :]
        seen = table[PHASED, rows, :], table[PHASED + 1, rows, :]
        next_run = cos_sin(east * (2.0 * RUN_ROWS / PIX))
        for f in range(FACETS):
            left = (shift_ref[0, f].astype(jnp.float32) + base_row) * (1.0 / PIX)
            right = (shift_ref[1, f].astype(jnp.float32) - 0.5) * (1.0 / PIX)
            phased = rotate(seen, cos_sin(frac(east * left) + frac(north * right)))
            for r in range(RUNS):
                if r:
                    phased = rotate(phased, next_run)
                at = PHASED + 2 * (f * RUNS + r)
                table[at, rows, :], table[at + 1, rows, :] = phased
        table[C64N, rows, :], table[S64N, rows, :] = cos_sin(north * (64.0 / PIX))
        for place, turns in enumerate((east, north)):
            first = now = cos_sin(turns * (0.5 / PIX))
            step = rotate(first, first)
            twice = 2.0 * step[0]
            before = now[0], -now[1]
            for j in range(8):
                if j:
                    before, now = now, tuple(twice * b - a for a, b in zip(before, now))
                for part in range(2):
                    starts[place * 2 + part, pl.ds(i * 64 + j, 8, stride=8), :] = now[part]
            t = (C8E, C8N)[place]
            table[t, rows, :], table[t + 1, rows, :] = rotate(now, first)

    panels = [panels[i : i + 4] for i in range(0, len(panels), 4)]
    for block, (left_cos, left_sin, right_cos, right_sin) in enumerate(panels):

        def row(i):
            return jnp.broadcast_to(table[i, block : block + 1, :], (8, LANES))

        def put(ref, at, first, second):
            ref[at : at + 16, :] = jnp.concatenate([first, second], axis=0).astype(jnp.bfloat16)

        here = slice(block * 8, (block + 1) * 8)
        base = starts[0, here, :], starts[1, here, :]
        turn = (row(C8E), row(S8E))
        wave = [base, rotate(base, turn)]
        twice = 2.0 * turn[0]
        for _ in range(2, RUN_HALF // 8):
            wave.append(tuple(twice * b - a for a, b in zip(wave[-2], wave[-1])))
        for f in range(FACETS):
            for r in range(RUNS):
                index = PHASED + 2 * (f * RUNS + r)
                real, imag = row(index), row(index + 1)
                at = (f * RUNS + r) * RUN_HALF
                for j in range(0, RUN_HALF // 8, 2):
                    (c0, s0), (c1, s1) = wave[j], wave[j + 1]
                    put(left_cos, at + j * 8, real * c0, real * c1)
                    put(left_cos, at + HALF + j * 8, imag * s0, imag * s1)
                    put(left_sin, at + j * 8, real * s0, real * s1)
                    put(left_sin, at + HALF + j * 8, imag * c0, imag * c1)

        start = starts[2, here, :], starts[3, here, :]
        turn = (row(C8N), row(S8N))
        next_run = (row(C64N), row(S64N))
        anchors = [(start, rotate(start, turn))]
        anchors.append(tuple(rotate(u, next_run) for u in anchors[0]))
        twice = 2.0 * next_run[0]
        for _ in range(2, RUNS):
            anchors.append(
                tuple(
                    tuple(twice * b - a for a, b in zip(old, new))
                    for old, new in zip(anchors[-2], anchors[-1])
                )
            )
        twice = 2.0 * turn[0]
        for r, (first, second) in enumerate(anchors):
            for part, ref in enumerate((right_cos, right_sin)):
                before, now = first[part], second[part]
                for j in range(0, STEPS, 2):
                    if j:
                        before = twice * now - before
                        now = twice * before - now
                    put(ref, r * RUN_ROWS + j * 8, before, now)

    left_cos, left_sin, right_cos, right_sin = (
        jnp.concatenate([ref[...] for ref in refs], axis=1) for refs in zip(*panels)
    )
    contract = (((1,), (1,)), ((), ()))
    for left, right in ((left_cos, right_cos), (left_sin, right_sin)):
        yield lax.dot_general(left, right, contract, preferred_element_type=jnp.float32)


def combine_kernel(scale, place_ref, data_ref, out_ref):
    shape = (OUT_ROWS, PEERS * OUT_ROWS)
    out_row = lax.broadcasted_iota(jnp.int32, shape, 0)
    sent_row = lax.broadcasted_iota(jnp.int32, shape, 1) % OUT_ROWS
    wanted = jnp.where(place_ref[0] < 2, OUT_ROWS - 1 - out_row, out_row)
    pick = (sent_row == wanted).astype(jnp.bfloat16)
    total = jnp.dot(pick, data_ref[...].reshape(PEERS * OUT_ROWS, FACETS * PIX), preferred_element_type=jnp.float32) * scale
    flip = (
        lax.broadcasted_iota(jnp.int32, (HALF, HALF), 0)
        + lax.broadcasted_iota(jnp.int32, (HALF, HALF), 1)
        == HALF - 1
    ).astype(jnp.bfloat16)
    evens = [total[:, f * PIX : f * PIX + HALF] for f in range(FACETS)]
    odds = [total[:, f * PIX + HALF : (f + 1) * PIX] for f in range(FACETS)]
    rest = jnp.concatenate([even + odd for even, odd in zip(evens, odds)], axis=0)
    pieces = []
    for _ in range(3):
        pieces.append(rest.astype(jnp.bfloat16))
        rest = rest - pieces[-1].astype(jnp.float32)
    turned = jnp.dot(jnp.concatenate(pieces, axis=0), flip, preferred_element_type=jnp.float32)
    rows = FACETS * OUT_ROWS
    mirrored = turned[:rows] + turned[rows : 2 * rows] + turned[2 * rows :]
    for f in range(FACETS):
        out_ref[0, :, f * PIX : f * PIX + HALF] = mirrored[f * OUT_ROWS : (f + 1) * OUT_ROWS]
        out_ref[0, :, f * PIX + HALF : (f + 1) * PIX] = evens[f] - odds[f]


VMEM = pl.BlockSpec(memory_space=pltpu.VMEM)
SMEM = pl.BlockSpec(memory_space=pltpu.SMEM)


def pack(visibility, weights, positions, station_pairs):
    return pl.pallas_call(
        pack_kernel,
        out_shape=jax.ShapeDtypeStruct((GROUPS, 4 * READ_ROWS, LANES), jnp.float32),
        in_specs=[VMEM, VMEM, SMEM, SMEM],
        out_specs=VMEM,
        name="pack",
    )(visibility, weights, positions, station_pairs)


SUMS = (2, FACETS * HALF, HALF)
ROWS_COST = pl.CostEstimate(
    flops=2 * math.prod(SUMS) * BLOCKS * LANES, bytes_accessed=4 * math.prod(SUMS), transcendentals=0
)
TABLE_SCRATCH = pltpu.VMEM((TABLE, BLOCKS, LANES), jnp.float32)
START_SCRATCH = pltpu.VMEM((4, BLOCKS * 8, LANES), jnp.float32)
PANELS = [
    pltpu.VMEM((FACETS * HALF, LANES), jnp.bfloat16),
    pltpu.VMEM((FACETS * HALF, LANES), jnp.bfloat16),
    pltpu.VMEM((HALF, LANES), jnp.bfloat16),
    pltpu.VMEM((HALF, LANES), jnp.bfloat16),
] * BLOCKS
IMAGE_PARAMS = pltpu.CompilerParams(vmem_limit_bytes=32 * 1024 * 1024)


def first_sums(half, facet_shift, arrived):
    return pl.pallas_call(
        first_kernel,
        out_shape=jax.ShapeDtypeStruct(SUMS, jnp.float32),
        in_specs=[SMEM, SMEM, VMEM],
        out_specs=VMEM,
        scratch_shapes=[TABLE_SCRATCH, START_SCRATCH, *PANELS],
        compiler_params=IMAGE_PARAMS,
        cost_estimate=ROWS_COST,
        name="first_sums",
    )(half, facet_shift, arrived)


def make_images(half, facet_shift, arrived, earlier):
    return pl.pallas_call(
        last_kernel,
        out_shape=jax.ShapeDtypeStruct((PEERS, OUT_ROWS, FACETS * PIX), jnp.bfloat16),
        in_specs=[SMEM, SMEM, VMEM, VMEM],
        out_specs=VMEM,
        scratch_shapes=[
            TABLE_SCRATCH,
            START_SCRATCH,
            pltpu.VMEM(SUMS, jnp.float32),
            *PANELS,
        ],
        compiler_params=IMAGE_PARAMS,
        cost_estimate=ROWS_COST,
        name="images",
    )(half, facet_shift, arrived, earlier)


def combine(scale, place, parts):
    return pl.pallas_call(
        functools.partial(combine_kernel, scale),
        out_shape=jax.ShapeDtypeStruct((1, OUT_ROWS, FACETS * PIX), jnp.float32),
        in_specs=[SMEM, VMEM],
        out_specs=VMEM,
        compiler_params=pltpu.CompilerParams(vmem_limit_bytes=8 * 1024 * 1024),
        name="combine",
    )(place, parts)


def body(visibility, weights, positions, station_pairs, facet_shift):
    half = lax.axis_index("zh").astype(jnp.int32).reshape(1)
    place = lax.axis_index("x").astype(jnp.int32).reshape(1)
    packed = pack(visibility, weights, positions, station_pairs)
    own = lax.all_to_all(packed, "chan", split_axis=0, concat_axis=0, tiled=True)
    other = lax.ppermute(own, "zh", [(h, HALVES - 1 - h) for h in range(HALVES)])
    earlier = first_sums(half, facet_shift, own)
    images = make_images(half, facet_shift, other, earlier)
    parts = lax.all_to_all(
        images, ("y", "x"), split_axis=0, concat_axis=0, tiled=True
    )
    scale = 1.0 / math.sqrt(READ_ROWS * GROUPS * 32 * LANES)
    return combine(scale, place, parts)


def solution(mesh):
    fine = Mesh(mesh.devices.reshape(GROUPS, 4, HALVES, 4), ("chan", "y", "zh", "x"))
    line = ("y", "zh", "x")
    in_specs = (
        P(None, ("chan", *line), None),
        P(("chan", *line), None),
        P(),
        P(None, ("chan", *line)),
        P(),
    )
    out_specs = P("chan", line, None)
    return jax.shard_map(body, mesh=fine, in_specs=in_specs, out_specs=out_specs, check_vma=False)
```

```python
import functools
import math

import jax
import jax.numpy as jnp
from jax import lax
from jax.experimental import pallas as pl
from jax.experimental.pallas import tpu as pltpu
from jax.sharding import Mesh, PartitionSpec as P

PIX = 512
HALF = PIX // 2
FACETS = 2
CHANNELS = 1024
GROUPS = 8
LANES = 128
READ_ROWS = 4
RUN_ROWS = 64
RUNS = 4
STEPS = RUN_ROWS // 8
RUN_HALF = RUN_ROWS // 2
HALVES = 2
SOURCES = GROUPS * HALVES
BLOCKS = SOURCES * READ_ROWS
PEERS = 16
OUT_ROWS = 16
COS_COEF = (
    1.0, -19.739208221435547, 64.93939208984375, -85.45665740966797,
    60.242130279541016, -26.4046688079834, 7.800131797790527, -1.4531123638153076,
)
SIN_COEF = (
    6.2831854820251465, -41.34170150756836, 81.60513305664062, -76.70301818847656,
    42.02592849731445, -14.899847984313965, 3.238137722015381,
)


def poly(coef, z):
    total = jnp.full_like(z, coef[-1])
    for c in coef[-2::-1]:
        total = total * z + c
    return total


def frac(turns):
    return turns - jnp.floor(turns + 0.5)


def cos_sin_reduced(r):
    z = r * r
    return poly(COS_COEF, z), poly(SIN_COEF, z) * r


def cos_sin(turns):
    return cos_sin_reduced(frac(turns))


def pack_kernel(vis_ref, weight_ref, pos_ref, pair_ref, out_ref):
    weight = weight_ref[...].astype(jnp.float32)
    real = weight * vis_ref[0].astype(jnp.float32)
    imag = weight * vis_ref[1].astype(jnp.float32)
    shape = (READ_ROWS, CHANNELS)
    channel = lax.broadcasted_iota(jnp.int32, shape, 1).astype(jnp.float32)
    frequency = 1.0 + channel / CHANNELS
    row = lax.broadcasted_iota(jnp.int32, shape, 0)
    spans = []
    for axis in range(2):
        span = jnp.zeros(shape, jnp.float32)
        for b in range(READ_ROWS):
            value = pos_ref[axis, pair_ref[0, b]] - pos_ref[axis, pair_ref[1, b]]
            span = jnp.where(row == b, value, span)
        spans.append(span * frequency)
    for a, values in enumerate((real, imag, *spans)):
        for g in range(GROUPS):
            part = values[:, g * LANES : (g + 1) * LANES]
            for h in range(HALVES):
                out_ref[g * HALVES + h, a * READ_ROWS : (a + 1) * READ_ROWS, :] = part


PHASED = 0
EAST, NORTH, C8E, S8E, C8N, S8N, C64N, S64N, TABLE = range(2 * FACETS * RUNS, 2 * FACETS * RUNS + 9)


def rotate(u, turn):
    (ur, ui), (c, s) = u, turn
    return ur * c - ui * s, ur * s + ui * c


def image_kernel(half_ref, shift_ref, data_ref, out_ref, table, starts, acc, *panels):
    for i, sums in enumerate(image_sums(half_ref, shift_ref, data_ref, table, starts, panels)):
        acc[i] = sums
    for f in range(FACETS):
        for r in range(RUNS):
            at = (f * RUNS + r) * RUN_HALF
            for i in range(2):
                column = (f * 2 + i) * HALF
                for k in range(RUN_HALF // OUT_ROWS):
                    rows = slice(at + k * OUT_ROWS, at + (k + 1) * OUT_ROWS)
                    rows_imag = slice(at + HALF + k * OUT_ROWS, at + HALF + (k + 1) * OUT_ROWS)
                    a, b = acc[i, rows], acc[i, rows_imag]
                    below, above = (a - b, a + b) if i == 0 else (b + a, b - a)
                    for place, values in ((2 + k, below), (1 - k, above)):
                        out_ref[r * 4 + place, :, column : column + HALF] = values.astype(jnp.bfloat16)


def image_sums(half_ref, shift_ref, data_ref, table, starts, panels):
    for s in range(SOURCES):
        for a, t in enumerate((PHASED, PHASED + 1, EAST, NORTH)):
            table[t, s * READ_ROWS : (s + 1) * READ_ROWS, :] = data_ref[
                s, a * READ_ROWS : (a + 1) * READ_ROWS, :
            ]
    base_row = (half_ref[0] * RUN_ROWS - HALF).astype(jnp.float32) + (RUN_HALF - 0.5)

    for i in range(BLOCKS // 8):
        rows = slice(i * 8, (i + 1) * 8)
        east = table[EAST, rows, :]
        north = table[NORTH, rows, :]
        seen = table[PHASED, rows, :], table[PHASED + 1, rows, :]
        next_run = cos_sin(east * (2.0 * RUN_ROWS / PIX))
        for f in range(FACETS):
            left = (shift_ref[0, f].astype(jnp.float32) + base_row) * (1.0 / PIX)
            right = (shift_ref[1, f].astype(jnp.float32) - 0.5) * (1.0 / PIX)
            phased = rotate(seen, cos_sin(frac(east * left) + frac(north * right)))
            for r in range(RUNS):
                if r:
                    phased = rotate(phased, next_run)
                at = PHASED + 2 * (f * RUNS + r)
                table[at, rows, :], table[at + 1, rows, :] = phased
        table[C64N, rows, :], table[S64N, rows, :] = cos_sin(north * (64.0 / PIX))
        for place, turns in enumerate((east, north)):
            first = now = cos_sin(turns * (0.5 / PIX))
            step = rotate(first, first)
            twice = 2.0 * step[0]
            before = now[0], -now[1]
            for j in range(8):
                if j:
                    before, now = now, tuple(twice * b - a for a, b in zip(before, now))
                for part in range(2):
                    starts[place * 2 + part, pl.ds(i * 64 + j, 8, stride=8), :] = now[part]
            t = (C8E, C8N)[place]
            table[t, rows, :], table[t + 1, rows, :] = rotate(now, first)

    panels = [panels[i : i + 4] for i in range(0, len(panels), 4)]
    for block, (left_cos, left_sin, right_cos, right_sin) in enumerate(panels):

        def row(i):
            return jnp.broadcast_to(table[i, block : block + 1, :], (8, LANES))

        def put(ref, at, first, second):
            ref[at : at + 16, :] = jnp.concatenate([first, second], axis=0).astype(jnp.bfloat16)

        here = slice(block * 8, (block + 1) * 8)
        base = starts[0, here, :], starts[1, here, :]
        turn = (row(C8E), row(S8E))
        wave = [base, rotate(base, turn)]
        twice = 2.0 * turn[0]
        for _ in range(2, RUN_HALF // 8):
            wave.append(tuple(twice * b - a for a, b in zip(wave[-2], wave[-1])))
        for f in range(FACETS):
            for r in range(RUNS):
                index = PHASED + 2 * (f * RUNS + r)
                real, imag = row(index), row(index + 1)
                at = (f * RUNS + r) * RUN_HALF
                for j in range(0, RUN_HALF // 8, 2):
                    (c0, s0), (c1, s1) = wave[j], wave[j + 1]
                    put(left_cos, at + j * 8, real * c0, real * c1)
                    put(left_cos, at + HALF + j * 8, imag * s0, imag * s1)
                    put(left_sin, at + j * 8, real * s0, real * s1)
                    put(left_sin, at + HALF + j * 8, imag * c0, imag * c1)

        start = starts[2, here, :], starts[3, here, :]
        turn = (row(C8N), row(S8N))
        next_run = (row(C64N), row(S64N))
        anchors = [(start, rotate(start, turn))]
        anchors.append(tuple(rotate(u, next_run) for u in anchors[0]))
        twice = 2.0 * next_run[0]
        for _ in range(2, RUNS):
            anchors.append(
                tuple(
                    tuple(twice * b - a for a, b in zip(old, new))
                    for old, new in zip(anchors[-2], anchors[-1])
                )
            )
        twice = 2.0 * turn[0]
        for r, (first, second) in enumerate(anchors):
            for part, ref in enumerate((right_cos, right_sin)):
                before, now = first[part], second[part]
                for j in range(0, STEPS, 2):
                    if j:
                        before = twice * now - before
                        now = twice * before - now
                    put(ref, r * RUN_ROWS + j * 8, before, now)

    left_cos, left_sin, right_cos, right_sin = (
        jnp.concatenate([ref[...] for ref in refs], axis=1) for refs in zip(*panels)
    )
    contract = (((1,), (1,)), ((), ()))
    for left, right in ((left_cos, right_cos), (left_sin, right_sin)):
        yield lax.dot_general(left, right, contract, preferred_element_type=jnp.float32)


def combine_kernel(scale, place_ref, data_ref, out_ref):
    shape = (OUT_ROWS, PEERS * OUT_ROWS)
    out_row = lax.broadcasted_iota(jnp.int32, shape, 0)
    sent_row = lax.broadcasted_iota(jnp.int32, shape, 1) % OUT_ROWS
    wanted = jnp.where(place_ref[0] < 2, OUT_ROWS - 1 - out_row, out_row)
    pick = (sent_row == wanted).astype(jnp.bfloat16)
    total = jnp.dot(pick, data_ref[...].reshape(PEERS * OUT_ROWS, FACETS * PIX), preferred_element_type=jnp.float32) * scale
    flip = (
        lax.broadcasted_iota(jnp.int32, (HALF, HALF), 0)
        + lax.broadcasted_iota(jnp.int32, (HALF, HALF), 1)
        == HALF - 1
    ).astype(jnp.bfloat16)
    evens = [total[:, f * PIX : f * PIX + HALF] for f in range(FACETS)]
    odds = [total[:, f * PIX + HALF : (f + 1) * PIX] for f in range(FACETS)]
    rest = jnp.concatenate([even + odd for even, odd in zip(evens, odds)], axis=0)
    pieces = []
    for _ in range(3):
        pieces.append(rest.astype(jnp.bfloat16))
        rest = rest - pieces[-1].astype(jnp.float32)
    turned = jnp.dot(jnp.concatenate(pieces, axis=0), flip, preferred_element_type=jnp.float32)
    rows = FACETS * OUT_ROWS
    mirrored = turned[:rows] + turned[rows : 2 * rows] + turned[2 * rows :]
    for f in range(FACETS):
        out_ref[0, :, f * PIX : f * PIX + HALF] = mirrored[f * OUT_ROWS : (f + 1) * OUT_ROWS]
        out_ref[0, :, f * PIX + HALF : (f + 1) * PIX] = evens[f] - odds[f]


VMEM = pl.BlockSpec(memory_space=pltpu.VMEM)
SMEM = pl.BlockSpec(memory_space=pltpu.SMEM)


def pack(visibility, weights, positions, station_pairs):
    return pl.pallas_call(
        pack_kernel,
        out_shape=jax.ShapeDtypeStruct((SOURCES, 4 * READ_ROWS, LANES), jnp.float32),
        in_specs=[VMEM, VMEM, SMEM, SMEM],
        out_specs=VMEM,
        name="pack",
    )(visibility, weights, positions, station_pairs)


SUMS = (2, FACETS * HALF, HALF)
ROWS_COST = pl.CostEstimate(
    flops=2 * math.prod(SUMS) * BLOCKS * LANES, bytes_accessed=4 * math.prod(SUMS), transcendentals=0
)
TABLE_SCRATCH = pltpu.VMEM((TABLE, BLOCKS, LANES), jnp.float32)
START_SCRATCH = pltpu.VMEM((4, BLOCKS * 8, LANES), jnp.float32)
PANELS = [
    pltpu.VMEM((FACETS * HALF, LANES), jnp.bfloat16),
    pltpu.VMEM((FACETS * HALF, LANES), jnp.bfloat16),
    pltpu.VMEM((HALF, LANES), jnp.bfloat16),
    pltpu.VMEM((HALF, LANES), jnp.bfloat16),
] * BLOCKS
IMAGE_PARAMS = pltpu.CompilerParams(vmem_limit_bytes=48 * 1024 * 1024)


def make_images(half, facet_shift, arrived):
    return pl.pallas_call(
        image_kernel,
        out_shape=jax.ShapeDtypeStruct((PEERS, OUT_ROWS, FACETS * PIX), jnp.bfloat16),
        in_specs=[SMEM, SMEM, VMEM],
        out_specs=VMEM,
        scratch_shapes=[
            TABLE_SCRATCH,
            START_SCRATCH,
            pltpu.VMEM(SUMS, jnp.float32),
            *PANELS,
        ],
        compiler_params=IMAGE_PARAMS,
        cost_estimate=ROWS_COST,
        name="images",
    )(half, facet_shift, arrived)


def combine(scale, place, parts):
    return pl.pallas_call(
        functools.partial(combine_kernel, scale),
        out_shape=jax.ShapeDtypeStruct((1, OUT_ROWS, FACETS * PIX), jnp.float32),
        in_specs=[SMEM, VMEM],
        out_specs=VMEM,
        compiler_params=pltpu.CompilerParams(vmem_limit_bytes=8 * 1024 * 1024),
        name="combine",
    )(place, parts)


def body(visibility, weights, positions, station_pairs, facet_shift):
    half = lax.axis_index("zh").astype(jnp.int32).reshape(1)
    place = lax.axis_index("x").astype(jnp.int32).reshape(1)
    packed = pack(visibility, weights, positions, station_pairs)
    arrived = lax.all_to_all(packed, ("chan", "zh"), split_axis=0, concat_axis=0, tiled=True)
    images = make_images(half, facet_shift, arrived)
    parts = lax.all_to_all(
        images, ("y", "x"), split_axis=0, concat_axis=0, tiled=True
    )
    scale = 1.0 / math.sqrt(READ_ROWS * GROUPS * 32 * LANES)
    return combine(scale, place, parts)


def solution(mesh):
    fine = Mesh(mesh.devices.reshape(GROUPS, 4, HALVES, 4), ("chan", "y", "zh", "x"))
    line = ("y", "zh", "x")
    in_specs = (
        P(None, ("chan", *line), None),
        P(("chan", *line), None),
        P(),
        P(None, ("chan", *line)),
        P(),
    )
    out_specs = P("chan", line, None)
    return jax.shard_map(body, mesh=fine, in_specs=in_specs, out_specs=out_specs, check_vma=False)
```

```python
import functools
import math

import jax
import jax.numpy as jnp
from jax import lax
from jax.experimental import pallas as pl
from jax.experimental.pallas import tpu as pltpu
from jax.sharding import Mesh, PartitionSpec as P

PIX = 512
HALF = PIX // 2
FACETS = 2
CHANNELS = 1024
GROUPS = 8
LANES = 128
READ_ROWS = 4
RUN_ROWS = 64
RUNS = 4
STEPS = RUN_ROWS // 8
RUN_HALF = RUN_ROWS // 2
HALVES = 2
BLOCKS = GROUPS * READ_ROWS
PEERS = 16
OUT_ROWS = 16
COS_COEF = (
    1.0, -19.739208221435547, 64.93939208984375, -85.45665740966797,
    60.242130279541016, -26.4046688079834, 7.800131797790527, -1.4531123638153076,
)
SIN_COEF = (
    6.2831854820251465, -41.34170150756836, 81.60513305664062, -76.70301818847656,
    42.02592849731445, -14.899847984313965, 3.238137722015381,
)


def poly(coef, z):
    total = jnp.full_like(z, coef[-1])
    for c in coef[-2::-1]:
        total = total * z + c
    return total


def frac(turns):
    return turns - jnp.floor(turns + 0.5)


def cos_sin_reduced(r):
    z = r * r
    return poly(COS_COEF, z), poly(SIN_COEF, z) * r


def cos_sin(turns):
    return cos_sin_reduced(frac(turns))


def pack_kernel(vis_ref, weight_ref, pos_ref, pair_ref, out_ref):
    weight = weight_ref[...].astype(jnp.float32)
    real = vis_ref[0].astype(jnp.float32)
    imag = vis_ref[1].astype(jnp.float32)
    shape = (READ_ROWS, LANES)
    row = lax.broadcasted_iota(jnp.int32, shape, 0)
    lane = lax.broadcasted_iota(jnp.int32, shape, 1)
    spans = jnp.zeros(shape, jnp.float32)
    for axis in range(2):
        rest = jnp.zeros(shape, jnp.float32)
        for b in range(READ_ROWS):
            value = pos_ref[axis, pair_ref[0, b]] - pos_ref[axis, pair_ref[1, b]]
            rest = jnp.where(row == b, value, rest)
        for i in range(3):
            piece = rest.astype(jnp.bfloat16).astype(jnp.float32)
            spans = jnp.where(lane == axis * 3 + i, piece, spans)
            rest = rest - piece
    for g in range(GROUPS):
        lanes = slice(g * LANES, (g + 1) * LANES)
        tile = [real[:, lanes], imag[:, lanes], weight[:, lanes], spans]
        out_ref[g] = jnp.concatenate(tile, axis=0).astype(jnp.bfloat16)


PHASED = 0
WEIGHT, SPANS, C8E, S8E, C8N, S8N, C64N, S64N, TABLE = range(2 * FACETS * RUNS, 2 * FACETS * RUNS + 9)


def rotate(u, turn):
    (ur, ui), (c, s) = u, turn
    return ur * c - ui * s, ur * s + ui * c


def first_kernel(place_ref, shift_ref, data_ref, out_ref, table, starts, *panels):
    for i, sums in enumerate(image_sums(place_ref, shift_ref, data_ref, table, starts, panels)):
        out_ref[i] = sums


def last_kernel(
    place_ref, shift_ref, data_ref, earlier_ref, out_ref, table, starts, acc, *panels
):
    for i, sums in enumerate(image_sums(place_ref, shift_ref, data_ref, table, starts, panels)):
        acc[i] = sums + earlier_ref[i]
    for f in range(FACETS):
        for r in range(RUNS):
            at = (f * RUNS + r) * RUN_HALF
            for i in range(2):
                column = (f * 2 + i) * HALF
                for k in range(RUN_HALF // OUT_ROWS):
                    rows = slice(at + k * OUT_ROWS, at + (k + 1) * OUT_ROWS)
                    rows_imag = slice(at + HALF + k * OUT_ROWS, at + HALF + (k + 1) * OUT_ROWS)
                    a, b = acc[i, rows], acc[i, rows_imag]
                    below, above = (a - b, a + b) if i == 0 else (b + a, b - a)
                    for place, values in ((2 + k, below), (1 - k, above)):
                        out_ref[r * 4 + place, :, column : column + HALF] = values.astype(jnp.bfloat16)


def image_sums(place_ref, shift_ref, data_ref, table, starts, panels):
    for s in range(GROUPS):
        tile = data_ref[s].astype(jnp.float32)
        for a, t in enumerate((PHASED, PHASED + 1, WEIGHT, SPANS)):
            table[t, s * READ_ROWS : (s + 1) * READ_ROWS, :] = tile[
                a * READ_ROWS : (a + 1) * READ_ROWS, :
            ]
    base_row = ((place_ref[0] % HALVES) * RUN_ROWS - HALF).astype(jnp.float32) + (RUN_HALF - 0.5)

    channel = (place_ref[0] // HALVES) * LANES + lax.broadcasted_iota(jnp.int32, (8, LANES), 1)
    frequency = 1.0 + channel.astype(jnp.float32) / CHANNELS
    for i in range(BLOCKS // 8):
        rows = slice(i * 8, (i + 1) * 8)
        spans = table[SPANS, rows, :]
        east, north = (
            (spans[:, a : a + 1] + spans[:, a + 1 : a + 2] + spans[:, a + 2 : a + 3]) * frequency
            for a in (0, 3)
        )
        weight = table[WEIGHT, rows, :]
        seen = weight * table[PHASED, rows, :], weight * table[PHASED + 1, rows, :]
        next_run = cos_sin(east * (2.0 * RUN_ROWS / PIX))
        for f in range(FACETS):
            left = (shift_ref[0, f].astype(jnp.float32) + base_row) * (1.0 / PIX)
            right = (shift_ref[1, f].astype(jnp.float32) - 0.5) * (1.0 / PIX)
            phased = rotate(seen, cos_sin(frac(east * left) + frac(north * right)))
            for r in range(RUNS):
                if r:
                    phased = rotate(phased, next_run)
                at = PHASED + 2 * (f * RUNS + r)
                table[at, rows, :], table[at + 1, rows, :] = phased
        table[C64N, rows, :], table[S64N, rows, :] = cos_sin(north * (64.0 / PIX))
        for place, turns in enumerate((east, north)):
            first = now = cos_sin(turns * (0.5 / PIX))
            step = rotate(first, first)
            twice = 2.0 * step[0]
            before = now[0], -now[1]
            for j in range(8):
                if j:
                    before, now = now, tuple(twice * b - a for a, b in zip(before, now))
                for part in range(2):
                    starts[place * 2 + part, pl.ds(i * 64 + j, 8, stride=8), :] = now[part]
            t = (C8E, C8N)[place]
            table[t, rows, :], table[t + 1, rows, :] = rotate(now, first)

    panels = [panels[i : i + 4] for i in range(0, len(panels), 4)]
    for block, (left_cos, left_sin, right_cos, right_sin) in enumerate(panels):

        def row(i):
            return jnp.broadcast_to(table[i, block : block + 1, :], (8, LANES))

        def put(ref, at, first, second):
            ref[at : at + 16, :] = jnp.concatenate([first, second], axis=0).astype(jnp.bfloat16)

        here = slice(block * 8, (block + 1) * 8)
        base = starts[0, here, :], starts[1, here, :]
        turn = (row(C8E), row(S8E))
        wave = [base, rotate(base, turn)]
        twice = 2.0 * turn[0]
        for _ in range(2, RUN_HALF // 8):
            wave.append(tuple(twice * b - a for a, b in zip(wave[-2], wave[-1])))
        for f in range(FACETS):
            for r in range(RUNS):
                index = PHASED + 2 * (f * RUNS + r)
                real, imag = row(index), row(index + 1)
                at = (f * RUNS + r) * RUN_HALF
                for j in range(0, RUN_HALF // 8, 2):
                    (c0, s0), (c1, s1) = wave[j], wave[j + 1]
                    put(left_cos, at + j * 8, real * c0, real * c1)
                    put(left_cos, at + HALF + j * 8, imag * s0, imag * s1)
                    put(left_sin, at + j * 8, real * s0, real * s1)
                    put(left_sin, at + HALF + j * 8, imag * c0, imag * c1)

        start = starts[2, here, :], starts[3, here, :]
        turn = (row(C8N), row(S8N))
        next_run = (row(C64N), row(S64N))
        anchors = [(start, rotate(start, turn))]
        anchors.append(tuple(rotate(u, next_run) for u in anchors[0]))
        twice = 2.0 * next_run[0]
        for _ in range(2, RUNS):
            anchors.append(
                tuple(
                    tuple(twice * b - a for a, b in zip(old, new))
                    for old, new in zip(anchors[-2], anchors[-1])
                )
            )
        twice = 2.0 * turn[0]
        for r, (first, second) in enumerate(anchors):
            for part, ref in enumerate((right_cos, right_sin)):
                before, now = first[part], second[part]
                for j in range(0, STEPS, 2):
                    if j:
                        before = twice * now - before
                        now = twice * before - now
                    put(ref, r * RUN_ROWS + j * 8, before, now)

    left_cos, left_sin, right_cos, right_sin = (
        jnp.concatenate([ref[...] for ref in refs], axis=1) for refs in zip(*panels)
    )
    contract = (((1,), (1,)), ((), ()))
    for left, right in ((left_cos, right_cos), (left_sin, right_sin)):
        yield lax.dot_general(left, right, contract, preferred_element_type=jnp.float32)


def combine_kernel(scale, place_ref, data_ref, out_ref):
    shape = (OUT_ROWS, PEERS * OUT_ROWS)
    out_row = lax.broadcasted_iota(jnp.int32, shape, 0)
    sent_row = lax.broadcasted_iota(jnp.int32, shape, 1) % OUT_ROWS
    wanted = jnp.where(place_ref[0] < 2, OUT_ROWS - 1 - out_row, out_row)
    pick = (sent_row == wanted).astype(jnp.bfloat16)
    total = jnp.dot(pick, data_ref[...].reshape(PEERS * OUT_ROWS, FACETS * PIX), preferred_element_type=jnp.float32) * scale
    flip = (
        lax.broadcasted_iota(jnp.int32, (HALF, HALF), 0)
        + lax.broadcasted_iota(jnp.int32, (HALF, HALF), 1)
        == HALF - 1
    ).astype(jnp.bfloat16)
    evens = [total[:, f * PIX : f * PIX + HALF] for f in range(FACETS)]
    odds = [total[:, f * PIX + HALF : (f + 1) * PIX] for f in range(FACETS)]
    rest = jnp.concatenate([even + odd for even, odd in zip(evens, odds)], axis=0)
    pieces = []
    for _ in range(3):
        pieces.append(rest.astype(jnp.bfloat16))
        rest = rest - pieces[-1].astype(jnp.float32)
    turned = jnp.dot(jnp.concatenate(pieces, axis=0), flip, preferred_element_type=jnp.float32)
    rows = FACETS * OUT_ROWS
    mirrored = turned[:rows] + turned[rows : 2 * rows] + turned[2 * rows :]
    for f in range(FACETS):
        out_ref[0, :, f * PIX : f * PIX + HALF] = mirrored[f * OUT_ROWS : (f + 1) * OUT_ROWS]
        out_ref[0, :, f * PIX + HALF : (f + 1) * PIX] = evens[f] - odds[f]


VMEM = pl.BlockSpec(memory_space=pltpu.VMEM)
SMEM = pl.BlockSpec(memory_space=pltpu.SMEM)


def pack(visibility, weights, positions, station_pairs):
    return pl.pallas_call(
        pack_kernel,
        out_shape=jax.ShapeDtypeStruct((GROUPS, 4 * READ_ROWS, LANES), jnp.bfloat16),
        in_specs=[VMEM, VMEM, SMEM, SMEM],
        out_specs=VMEM,
        name="pack",
    )(visibility, weights, positions, station_pairs)


SUMS = (2, FACETS * HALF, HALF)
ROWS_COST = pl.CostEstimate(
    flops=2 * math.prod(SUMS) * BLOCKS * LANES, bytes_accessed=4 * math.prod(SUMS), transcendentals=0
)
TABLE_SCRATCH = pltpu.VMEM((TABLE, BLOCKS, LANES), jnp.float32)
START_SCRATCH = pltpu.VMEM((4, BLOCKS * 8, LANES), jnp.float32)
PANELS = [
    pltpu.VMEM((FACETS * HALF, LANES), jnp.bfloat16),
    pltpu.VMEM((FACETS * HALF, LANES), jnp.bfloat16),
    pltpu.VMEM((HALF, LANES), jnp.bfloat16),
    pltpu.VMEM((HALF, LANES), jnp.bfloat16),
] * BLOCKS
IMAGE_PARAMS = pltpu.CompilerParams(vmem_limit_bytes=32 * 1024 * 1024)


def first_sums(half, facet_shift, arrived):
    return pl.pallas_call(
        first_kernel,
        out_shape=jax.ShapeDtypeStruct(SUMS, jnp.float32),
        in_specs=[SMEM, SMEM, VMEM],
        out_specs=VMEM,
        scratch_shapes=[TABLE_SCRATCH, START_SCRATCH, *PANELS],
        compiler_params=IMAGE_PARAMS,
        cost_estimate=ROWS_COST,
        name="first_sums",
    )(half, facet_shift, arrived)


def make_images(half, facet_shift, arrived, earlier):
    return pl.pallas_call(
        last_kernel,
        out_shape=jax.ShapeDtypeStruct((PEERS, OUT_ROWS, FACETS * PIX), jnp.bfloat16),
        in_specs=[SMEM, SMEM, VMEM, VMEM],
        out_specs=VMEM,
        scratch_shapes=[
            TABLE_SCRATCH,
            START_SCRATCH,
            pltpu.VMEM(SUMS, jnp.float32),
            *PANELS,
        ],
        compiler_params=IMAGE_PARAMS,
        cost_estimate=ROWS_COST,
        name="images",
    )(half, facet_shift, arrived, earlier)


def combine(scale, place, parts):
    return pl.pallas_call(
        functools.partial(combine_kernel, scale),
        out_shape=jax.ShapeDtypeStruct((1, OUT_ROWS, FACETS * PIX), jnp.float32),
        in_specs=[SMEM, VMEM],
        out_specs=VMEM,
        compiler_params=pltpu.CompilerParams(vmem_limit_bytes=8 * 1024 * 1024),
        name="combine",
    )(place, parts)


def body(visibility, weights, positions, station_pairs, facet_shift):
    half = (lax.axis_index("chan") * HALVES + lax.axis_index("zh")).astype(jnp.int32).reshape(1)
    place = lax.axis_index("x").astype(jnp.int32).reshape(1)
    packed = pack(visibility, weights, positions, station_pairs)
    own = lax.all_to_all(packed, "chan", split_axis=0, concat_axis=0, tiled=True)
    other = lax.ppermute(own, "zh", [(h, HALVES - 1 - h) for h in range(HALVES)])
    earlier = first_sums(half, facet_shift, own)
    images = make_images(half, facet_shift, other, earlier)
    parts = lax.all_to_all(
        images, ("y", "x"), split_axis=0, concat_axis=0, tiled=True
    )
    scale = 1.0 / math.sqrt(READ_ROWS * GROUPS * 32 * LANES)
    return combine(scale, place, parts)


def solution(mesh):
    fine = Mesh(mesh.devices.reshape(GROUPS, 4, HALVES, 4), ("chan", "y", "zh", "x"))
    line = ("y", "zh", "x")
    in_specs = (
        P(None, ("chan", *line), None),
        P(("chan", *line), None),
        P(),
        P(None, ("chan", *line)),
        P(),
    )
    out_specs = P("chan", line, None)
    return jax.shard_map(body, mesh=fine, in_specs=in_specs, out_specs=out_specs, check_vma=False)
```

```python
import functools
import math

import jax
import jax.numpy as jnp
from jax import lax
from jax.experimental import pallas as pl
from jax.experimental.pallas import tpu as pltpu
from jax.sharding import Mesh, PartitionSpec as P

PIX = 512
HALF = PIX // 2
FACETS = 2
CHANNELS = 1024
GROUPS = 8
LANES = 128
READ_ROWS = 4
HALVES = 2
PAIRS = 2
ROWS_Y = 4
OUT_ROWS = 16
RUNS = ROWS_Y * PAIRS
RUN_HALF = OUT_ROWS // 2
PART_ROWS = FACETS * RUNS * RUN_HALF
COLUMN_RUN = 64
COLUMN_RUNS = HALF // COLUMN_RUN
STEPS = COLUMN_RUN // 8
SOURCES = GROUPS * PAIRS
BLOCKS = SOURCES * READ_ROWS
COS_COEF = (
    1.0, -19.739208221435547, 64.93939208984375, -85.45665740966797,
    60.242130279541016, -26.4046688079834, 7.800131797790527, -1.4531123638153076,
)
SIN_COEF = (
    6.2831854820251465, -41.34170150756836, 81.60513305664062, -76.70301818847656,
    42.02592849731445, -14.899847984313965, 3.238137722015381,
)


def poly(coef, z):
    total = jnp.full_like(z, coef[-1])
    for c in coef[-2::-1]:
        total = total * z + c
    return total


def frac(turns):
    return turns - jnp.floor(turns + 0.5)


def cos_sin_reduced(r):
    z = r * r
    return poly(COS_COEF, z), poly(SIN_COEF, z) * r


def cos_sin(turns):
    return cos_sin_reduced(frac(turns))


def pack_kernel(vis_ref, weight_ref, pos_ref, pair_ref, out_ref):
    weight = weight_ref[...].astype(jnp.float32)
    real = vis_ref[0].astype(jnp.float32)
    imag = vis_ref[1].astype(jnp.float32)
    shape = (READ_ROWS, LANES)
    row = lax.broadcasted_iota(jnp.int32, shape, 0)
    lane = lax.broadcasted_iota(jnp.int32, shape, 1)
    spans = jnp.zeros(shape, jnp.float32)
    for axis in range(2):
        rest = jnp.zeros(shape, jnp.float32)
        for b in range(READ_ROWS):
            value = pos_ref[axis, pair_ref[0, b]] - pos_ref[axis, pair_ref[1, b]]
            rest = jnp.where(row == b, value, rest)
        for i in range(3):
            piece = rest.astype(jnp.bfloat16).astype(jnp.float32)
            spans = jnp.where(lane == axis * 3 + i, piece, spans)
            rest = rest - piece
    for g in range(GROUPS):
        lanes = slice(g * LANES, (g + 1) * LANES)
        tile = [real[:, lanes], imag[:, lanes], weight[:, lanes], spans]
        tile = jnp.concatenate(tile, axis=0).astype(jnp.bfloat16)
        for pair in range(PAIRS):
            out_ref[g * PAIRS + pair] = tile


PHASED = 0
WEIGHT, SPANS, C8N, S8N, C64N, S64N, TABLE = range(2 * FACETS * RUNS, 2 * FACETS * RUNS + 7)


def rotate(u, turn):
    (ur, ui), (c, s) = u, turn
    return ur * c - ui * s, ur * s + ui * c


def first_kernel(place_ref, shift_ref, data_ref, out_ref, table, starts, *panels):
    for i, sums in enumerate(image_sums(place_ref, shift_ref, data_ref, table, starts, panels)):
        out_ref[i] = sums


def last_kernel(
    place_ref, shift_ref, data_ref, earlier_ref, out_ref, table, starts, acc, *panels
):
    for i, sums in enumerate(image_sums(place_ref, shift_ref, data_ref, table, starts, panels)):
        acc[i] = sums + earlier_ref[i]
    for f in range(FACETS):
        for r in range(RUNS):
            at = (f * RUNS + r) * RUN_HALF
            for i in range(2):
                column = (f * 2 + i) * HALF
                a = acc[i, at : at + RUN_HALF]
                b = acc[i, PART_ROWS + at : PART_ROWS + at + RUN_HALF]
                above, below = (a + b, a - b) if i == 0 else (b - a, b + a)
                out_ref[r, :, column : column + HALF] = jnp.concatenate(
                    [above, below], axis=0
                ).astype(jnp.bfloat16)


def image_sums(place_ref, shift_ref, data_ref, table, starts, panels):
    for s in range(SOURCES):
        tile = data_ref[s].astype(jnp.float32)
        for a, t in enumerate((PHASED, PHASED + 1, WEIGHT, SPANS)):
            table[t, s * READ_ROWS : (s + 1) * READ_ROWS, :] = tile[
                a * READ_ROWS : (a + 1) * READ_ROWS, :
            ]
    pair = place_ref[0] % PAIRS
    half = (place_ref[0] // PAIRS) % HALVES
    group = place_ref[0] // (PAIRS * HALVES)
    first_row = half * PAIRS * (PAIRS * OUT_ROWS) + pair * OUT_ROWS - HALF
    base_row = first_row.astype(jnp.float32) + (RUN_HALF - 0.5)
    channel = group * LANES + lax.broadcasted_iota(jnp.int32, (8, LANES), 1)
    frequency = 1.0 + channel.astype(jnp.float32) / CHANNELS
    for i in range(BLOCKS // 8):
        rows = slice(i * 8, (i + 1) * 8)
        spans = table[SPANS, rows, :]
        east, north = (
            (spans[:, a : a + 1] + spans[:, a + 1 : a + 2] + spans[:, a + 2 : a + 3]) * frequency
            for a in (0, 3)
        )
        weight = table[WEIGHT, rows, :]
        seen = weight * table[PHASED, rows, :], weight * table[PHASED + 1, rows, :]
        to_next_y = cos_sin(east * (HALVES * PAIRS * PAIRS * OUT_ROWS / PIX))
        to_next_x = cos_sin(east * (PAIRS * OUT_ROWS / PIX))
        for f in range(FACETS):
            left = (shift_ref[0, f].astype(jnp.float32) + base_row) * (1.0 / PIX)
            right = (shift_ref[1, f].astype(jnp.float32) - 0.5) * (1.0 / PIX)
            phased = rotate(seen, cos_sin(frac(east * left) + frac(north * right)))
            for y in range(ROWS_Y):
                if y:
                    phased = rotate(phased, to_next_y)
                for x, values in enumerate((phased, rotate(phased, to_next_x))):
                    at = PHASED + 2 * (f * RUNS + y * PAIRS + x)
                    table[at, rows, :], table[at + 1, rows, :] = values
        table[C64N, rows, :], table[S64N, rows, :] = cos_sin(north * (64.0 / PIX))
        for place, turns in enumerate((east, north)):
            first = now = cos_sin(turns * (0.5 / PIX))
            step = rotate(first, first)
            twice = 2.0 * step[0]
            before = now[0], -now[1]
            for j in range(8):
                if j:
                    before, now = now, tuple(twice * b - a for a, b in zip(before, now))
                for part in range(2):
                    starts[place * 2 + part, pl.ds(i * 64 + j, 8, stride=8), :] = now[part]
            if place:
                table[C8N, rows, :], table[S8N, rows, :] = rotate(now, first)

    panels = [panels[i : i + 4] for i in range(0, len(panels), 4)]
    for block, (left_cos, left_sin, right_cos, right_sin) in enumerate(panels):

        def row(i):
            return jnp.broadcast_to(table[i, block : block + 1, :], (8, LANES))

        def put(ref, at, first, second):
            ref[at : at + 16, :] = jnp.concatenate([first, second], axis=0).astype(jnp.bfloat16)

        here = slice(block * 8, (block + 1) * 8)
        cos, sin = starts[0, here, :], starts[1, here, :]
        for pair in range(0, FACETS * RUNS, 2):
            (r0, i0), (r1, i1) = (
                (row(PHASED + 2 * k), row(PHASED + 2 * k + 1)) for k in (pair, pair + 1)
            )
            at = pair * RUN_HALF
            put(left_cos, at, r0 * cos, r1 * cos)
            put(left_cos, PART_ROWS + at, i0 * sin, i1 * sin)
            put(left_sin, at, r0 * sin, r1 * sin)
            put(left_sin, PART_ROWS + at, i0 * cos, i1 * cos)

        start = starts[2, here, :], starts[3, here, :]
        turn = (row(C8N), row(S8N))
        next_run = (row(C64N), row(S64N))
        anchors = [(start, rotate(start, turn))]
        anchors.append(tuple(rotate(u, next_run) for u in anchors[0]))
        twice = 2.0 * next_run[0]
        for _ in range(2, COLUMN_RUNS):
            anchors.append(
                tuple(
                    tuple(twice * b - a for a, b in zip(old, new))
                    for old, new in zip(anchors[-2], anchors[-1])
                )
            )
        twice = 2.0 * turn[0]
        for r, (first, second) in enumerate(anchors):
            for part, ref in enumerate((right_cos, right_sin)):
                before, now = first[part], second[part]
                for j in range(0, STEPS, 2):
                    if j:
                        before = twice * now - before
                        now = twice * before - now
                    put(ref, r * COLUMN_RUN + j * 8, before, now)

    left_cos, left_sin, right_cos, right_sin = (
        jnp.concatenate([ref[...] for ref in refs], axis=1) for refs in zip(*panels)
    )
    contract = (((1,), (1,)), ((), ()))
    for left, right in ((left_cos, right_cos), (left_sin, right_sin)):
        yield lax.dot_general(left, right, contract, preferred_element_type=jnp.float32)


def combine_kernel(scale, data_ref, out_ref):
    shape = (OUT_ROWS, RUNS * OUT_ROWS)
    out_row = lax.broadcasted_iota(jnp.int32, shape, 0)
    sent_row = lax.broadcasted_iota(jnp.int32, shape, 1) % OUT_ROWS
    wanted = jnp.where(out_row < RUN_HALF, RUN_HALF - 1 - out_row, out_row)
    pick = (sent_row == wanted).astype(jnp.bfloat16)
    data = data_ref[...].reshape(RUNS * OUT_ROWS, FACETS * PIX)
    total = jnp.dot(pick, data, preferred_element_type=jnp.float32) * scale
    flip = (
        lax.broadcasted_iota(jnp.int32, (HALF, HALF), 0)
        + lax.broadcasted_iota(jnp.int32, (HALF, HALF), 1)
        == HALF - 1
    ).astype(jnp.bfloat16)
    evens = [total[:, f * PIX : f * PIX + HALF] for f in range(FACETS)]
    odds = [total[:, f * PIX + HALF : (f + 1) * PIX] for f in range(FACETS)]
    rest = jnp.concatenate([even + odd for even, odd in zip(evens, odds)], axis=0)
    pieces = []
    for _ in range(3):
        pieces.append(rest.astype(jnp.bfloat16))
        rest = rest - pieces[-1].astype(jnp.float32)
    turned = jnp.dot(jnp.concatenate(pieces, axis=0), flip, preferred_element_type=jnp.float32)
    rows = FACETS * OUT_ROWS
    mirrored = turned[:rows] + turned[rows : 2 * rows] + turned[2 * rows :]
    for f in range(FACETS):
        out_ref[0, :, f * PIX : f * PIX + HALF] = mirrored[f * OUT_ROWS : (f + 1) * OUT_ROWS]
        out_ref[0, :, f * PIX + HALF : (f + 1) * PIX] = evens[f] - odds[f]


VMEM = pl.BlockSpec(memory_space=pltpu.VMEM)
SMEM = pl.BlockSpec(memory_space=pltpu.SMEM)


def pack(visibility, weights, positions, station_pairs):
    return pl.pallas_call(
        pack_kernel,
        out_shape=jax.ShapeDtypeStruct((SOURCES, 4 * READ_ROWS, LANES), jnp.bfloat16),
        in_specs=[VMEM, VMEM, SMEM, SMEM],
        out_specs=VMEM,
        name="pack",
    )(visibility, weights, positions, station_pairs)


SUMS = (2, 2 * PART_ROWS, HALF)
ROWS_COST = pl.CostEstimate(
    flops=2 * math.prod(SUMS) * BLOCKS * LANES, bytes_accessed=4 * math.prod(SUMS), transcendentals=0
)
TABLE_SCRATCH = pltpu.VMEM((TABLE, BLOCKS, LANES), jnp.float32)
START_SCRATCH = pltpu.VMEM((4, BLOCKS * 8, LANES), jnp.float32)
PANELS = [
    pltpu.VMEM((2 * PART_ROWS, LANES), jnp.bfloat16),
    pltpu.VMEM((2 * PART_ROWS, LANES), jnp.bfloat16),
    pltpu.VMEM((HALF, LANES), jnp.bfloat16),
    pltpu.VMEM((HALF, LANES), jnp.bfloat16),
] * BLOCKS
IMAGE_PARAMS = pltpu.CompilerParams(vmem_limit_bytes=32 * 1024 * 1024)


def first_sums(half, facet_shift, arrived):
    return pl.pallas_call(
        first_kernel,
        out_shape=jax.ShapeDtypeStruct(SUMS, jnp.float32),
        in_specs=[SMEM, SMEM, VMEM],
        out_specs=VMEM,
        scratch_shapes=[TABLE_SCRATCH, START_SCRATCH, *PANELS],
        compiler_params=IMAGE_PARAMS,
        cost_estimate=ROWS_COST,
        name="first_sums",
    )(half, facet_shift, arrived)


def make_images(half, facet_shift, arrived, earlier):
    return pl.pallas_call(
        last_kernel,
        out_shape=jax.ShapeDtypeStruct((RUNS, OUT_ROWS, FACETS * PIX), jnp.bfloat16),
        in_specs=[SMEM, SMEM, VMEM, VMEM],
        out_specs=VMEM,
        scratch_shapes=[
            TABLE_SCRATCH,
            START_SCRATCH,
            pltpu.VMEM(SUMS, jnp.float32),
            *PANELS,
        ],
        compiler_params=IMAGE_PARAMS,
        cost_estimate=ROWS_COST,
        name="images",
    )(half, facet_shift, arrived, earlier)


def combine(scale, parts):
    return pl.pallas_call(
        functools.partial(combine_kernel, scale),
        out_shape=jax.ShapeDtypeStruct((1, OUT_ROWS, FACETS * PIX), jnp.float32),
        in_specs=[VMEM],
        out_specs=VMEM,
        compiler_params=pltpu.CompilerParams(vmem_limit_bytes=8 * 1024 * 1024),
        name="combine",
    )(parts)


def body(visibility, weights, positions, station_pairs, facet_shift):
    place = lax.axis_index("chan") * HALVES + lax.axis_index("zh")
    place = (place * PAIRS + lax.axis_index("xl")).astype(jnp.int32).reshape(1)
    packed = pack(visibility, weights, positions, station_pairs)
    own = lax.all_to_all(packed, ("chan", "xl"), split_axis=0, concat_axis=0, tiled=True)
    other = lax.ppermute(own, "zh", [(h, HALVES - 1 - h) for h in range(HALVES)])
    earlier = first_sums(place, facet_shift, own)
    images = make_images(place, facet_shift, other, earlier)
    parts = lax.all_to_all(
        images, ("y", "xh"), split_axis=0, concat_axis=0, tiled=True
    )
    scale = 1.0 / math.sqrt(READ_ROWS * GROUPS * 32 * LANES)
    return combine(scale, parts)


def solution(mesh):
    shape = (GROUPS, ROWS_Y, HALVES, PAIRS, PAIRS)
    line = ("y", "zh", "xh", "xl")
    fine = Mesh(mesh.devices.reshape(shape), ("chan", *line))
    in_specs = (
        P(None, ("chan", *line), None),
        P(("chan", *line), None),
        P(),
        P(None, ("chan", *line)),
        P(),
    )
    out_specs = P("chan", line, None)
    return jax.shard_map(body, mesh=fine, in_specs=in_specs, out_specs=out_specs, check_vma=False)
```

```python
import functools
import math

import jax
import jax.numpy as jnp
from jax import lax
from jax.experimental import pallas as pl
from jax.experimental.pallas import tpu as pltpu
from jax.sharding import Mesh, PartitionSpec as P

PIX = 512
HALF = PIX // 2
FACETS = 2
CHANNELS = 1024
GROUPS = 8
LANES = 128
READ_ROWS = 4
RUN_ROWS = 64
RUNS = 4
STEPS = RUN_ROWS // 8
RUN_HALF = RUN_ROWS // 2
HALVES = 2
SOURCES = GROUPS * HALVES
BLOCKS = SOURCES * READ_ROWS
PEERS = 16
OUT_ROWS = 16
COS_COEF = (
    1.0, -19.739208221435547, 64.93939208984375, -85.45665740966797,
    60.242130279541016, -26.4046688079834, 7.800131797790527, -1.4531123638153076,
)
SIN_COEF = (
    6.2831854820251465, -41.34170150756836, 81.60513305664062, -76.70301818847656,
    42.02592849731445, -14.899847984313965, 3.238137722015381,
)


def poly(coef, z):
    total = jnp.full_like(z, coef[-1])
    for c in coef[-2::-1]:
        total = total * z + c
    return total


def frac(turns):
    return turns - jnp.floor(turns + 0.5)


def cos_sin_reduced(r):
    z = r * r
    return poly(COS_COEF, z), poly(SIN_COEF, z) * r


def cos_sin(turns):
    return cos_sin_reduced(frac(turns))


def pack_kernel(vis_ref, weight_ref, pos_ref, pair_ref, out_ref):
    weight = weight_ref[...].astype(jnp.float32)
    real = vis_ref[0].astype(jnp.float32)
    imag = vis_ref[1].astype(jnp.float32)
    shape = (READ_ROWS, LANES)
    row = lax.broadcasted_iota(jnp.int32, shape, 0)
    lane = lax.broadcasted_iota(jnp.int32, shape, 1)
    spans = jnp.zeros(shape, jnp.float32)
    for axis in range(2):
        rest = jnp.zeros(shape, jnp.float32)
        for b in range(READ_ROWS):
            value = pos_ref[axis, pair_ref[0, b]] - pos_ref[axis, pair_ref[1, b]]
            rest = jnp.where(row == b, value, rest)
        for i in range(3):
            piece = rest.astype(jnp.bfloat16).astype(jnp.float32)
            spans = jnp.where(lane == axis * 3 + i, piece, spans)
            rest = rest - piece
    for g in range(GROUPS):
        lanes = slice(g * LANES, (g + 1) * LANES)
        tile = [real[:, lanes], imag[:, lanes], weight[:, lanes], spans]
        tile = jnp.concatenate(tile, axis=0).astype(jnp.bfloat16)
        for h in range(HALVES):
            out_ref[g * HALVES + h] = tile


PHASED = 0
WEIGHT, SPANS, C8E, S8E, C8N, S8N, C64N, S64N, TABLE = range(2 * FACETS * RUNS, 2 * FACETS * RUNS + 9)


def rotate(u, turn):
    (ur, ui), (c, s) = u, turn
    return ur * c - ui * s, ur * s + ui * c


def image_kernel(place_ref, shift_ref, data_ref, out_ref, table, starts, acc, *panels):
    for i, sums in enumerate(image_sums(place_ref, shift_ref, data_ref, table, starts, panels)):
        acc[i] = sums
    for f in range(FACETS):
        for r in range(RUNS):
            at = (f * RUNS + r) * RUN_HALF
            for i in range(2):
                column = (f * 2 + i) * HALF
                for k in range(RUN_HALF // OUT_ROWS):
                    rows = slice(at + k * OUT_ROWS, at + (k + 1) * OUT_ROWS)
                    rows_imag = slice(at + HALF + k * OUT_ROWS, at + HALF + (k + 1) * OUT_ROWS)
                    a, b = acc[i, rows], acc[i, rows_imag]
                    below, above = (a - b, a + b) if i == 0 else (b + a, b - a)
                    for place, values in ((2 + k, below), (1 - k, above)):
                        out_ref[r * 4 + place, :, column : column + HALF] = values.astype(jnp.bfloat16)


def image_sums(place_ref, shift_ref, data_ref, table, starts, panels):
    for s in range(SOURCES):
        tile = data_ref[s].astype(jnp.float32)
        for a, t in enumerate((PHASED, PHASED + 1, WEIGHT, SPANS)):
            table[t, s * READ_ROWS : (s + 1) * READ_ROWS, :] = tile[
                a * READ_ROWS : (a + 1) * READ_ROWS, :
            ]
    base_row = ((place_ref[0] % HALVES) * RUN_ROWS - HALF).astype(jnp.float32) + (RUN_HALF - 0.5)

    channel = (place_ref[0] // HALVES) * LANES + lax.broadcasted_iota(jnp.int32, (8, LANES), 1)
    frequency = 1.0 + channel.astype(jnp.float32) / CHANNELS
    for i in range(BLOCKS // 8):
        rows = slice(i * 8, (i + 1) * 8)
        spans = table[SPANS, rows, :]
        east, north = (
            (spans[:, a : a + 1] + spans[:, a + 1 : a + 2] + spans[:, a + 2 : a + 3]) * frequency
            for a in (0, 3)
        )
        weight = table[WEIGHT, rows, :]
        seen = weight * table[PHASED, rows, :], weight * table[PHASED + 1, rows, :]
        next_run = cos_sin(east * (2.0 * RUN_ROWS / PIX))
        for f in range(FACETS):
            left = (shift_ref[0, f].astype(jnp.float32) + base_row) * (1.0 / PIX)
            right = (shift_ref[1, f].astype(jnp.float32) - 0.5) * (1.0 / PIX)
            phased = rotate(seen, cos_sin(frac(east * left) + frac(north * right)))
            for r in range(RUNS):
                if r:
                    phased = rotate(phased, next_run)
                at = PHASED + 2 * (f * RUNS + r)
                table[at, rows, :], table[at + 1, rows, :] = phased
        table[C64N, rows, :], table[S64N, rows, :] = cos_sin(north * (64.0 / PIX))
        for place, turns in enumerate((east, north)):
            first = now = cos_sin(turns * (0.5 / PIX))
            step = rotate(first, first)
            twice = 2.0 * step[0]
            before = now[0], -now[1]
            for j in range(8):
                if j:
                    before, now = now, tuple(twice * b - a for a, b in zip(before, now))
                for part in range(2):
                    starts[place * 2 + part, pl.ds(i * 64 + j, 8, stride=8), :] = now[part]
            t = (C8E, C8N)[place]
            table[t, rows, :], table[t + 1, rows, :] = rotate(now, first)

    panels = [panels[i : i + 4] for i in range(0, len(panels), 4)]
    for block, (left_cos, left_sin, right_cos, right_sin) in enumerate(panels):

        def row(i):
            return jnp.broadcast_to(table[i, block : block + 1, :], (8, LANES))

        def put(ref, at, first, second):
            ref[at : at + 16, :] = jnp.concatenate([first, second], axis=0).astype(jnp.bfloat16)

        here = slice(block * 8, (block + 1) * 8)
        base = starts[0, here, :], starts[1, here, :]
        turn = (row(C8E), row(S8E))
        wave = [base, rotate(base, turn)]
        twice = 2.0 * turn[0]
        for _ in range(2, RUN_HALF // 8):
            wave.append(tuple(twice * b - a for a, b in zip(wave[-2], wave[-1])))
        for f in range(FACETS):
            for r in range(RUNS):
                index = PHASED + 2 * (f * RUNS + r)
                real, imag = row(index), row(index + 1)
                at = (f * RUNS + r) * RUN_HALF
                for j in range(0, RUN_HALF // 8, 2):
                    (c0, s0), (c1, s1) = wave[j], wave[j + 1]
                    put(left_cos, at + j * 8, real * c0, real * c1)
                    put(left_cos, at + HALF + j * 8, imag * s0, imag * s1)
                    put(left_sin, at + j * 8, real * s0, real * s1)
                    put(left_sin, at + HALF + j * 8, imag * c0, imag * c1)

        start = starts[2, here, :], starts[3, here, :]
        turn = (row(C8N), row(S8N))
        next_run = (row(C64N), row(S64N))
        anchors = [(start, rotate(start, turn))]
        anchors.append(tuple(rotate(u, next_run) for u in anchors[0]))
        twice = 2.0 * next_run[0]
        for _ in range(2, RUNS):
            anchors.append(
                tuple(
                    tuple(twice * b - a for a, b in zip(old, new))
                    for old, new in zip(anchors[-2], anchors[-1])
                )
            )
        twice = 2.0 * turn[0]
        for r, (first, second) in enumerate(anchors):
            for part, ref in enumerate((right_cos, right_sin)):
                before, now = first[part], second[part]
                for j in range(0, STEPS, 2):
                    if j:
                        before = twice * now - before
                        now = twice * before - now
                    put(ref, r * RUN_ROWS + j * 8, before, now)

    left_cos, left_sin, right_cos, right_sin = (
        jnp.concatenate([ref[...] for ref in refs], axis=1) for refs in zip(*panels)
    )
    contract = (((1,), (1,)), ((), ()))
    for left, right in ((left_cos, right_cos), (left_sin, right_sin)):
        yield lax.dot_general(left, right, contract, preferred_element_type=jnp.float32)


def combine_kernel(scale, place_ref, data_ref, out_ref):
    shape = (OUT_ROWS, PEERS * OUT_ROWS)
    out_row = lax.broadcasted_iota(jnp.int32, shape, 0)
    sent_row = lax.broadcasted_iota(jnp.int32, shape, 1) % OUT_ROWS
    wanted = jnp.where(place_ref[0] < 2, OUT_ROWS - 1 - out_row, out_row)
    pick = (sent_row == wanted).astype(jnp.bfloat16)
    total = jnp.dot(pick, data_ref[...].reshape(PEERS * OUT_ROWS, FACETS * PIX), preferred_element_type=jnp.float32) * scale
    flip = (
        lax.broadcasted_iota(jnp.int32, (HALF, HALF), 0)
        + lax.broadcasted_iota(jnp.int32, (HALF, HALF), 1)
        == HALF - 1
    ).astype(jnp.bfloat16)
    evens = [total[:, f * PIX : f * PIX + HALF] for f in range(FACETS)]
    odds = [total[:, f * PIX + HALF : (f + 1) * PIX] for f in range(FACETS)]
    rest = jnp.concatenate([even + odd for even, odd in zip(evens, odds)], axis=0)
    pieces = []
    for _ in range(3):
        pieces.append(rest.astype(jnp.bfloat16))
        rest = rest - pieces[-1].astype(jnp.float32)
    turned = jnp.dot(jnp.concatenate(pieces, axis=0), flip, preferred_element_type=jnp.float32)
    rows = FACETS * OUT_ROWS
    mirrored = turned[:rows] + turned[rows : 2 * rows] + turned[2 * rows :]
    for f in range(FACETS):
        out_ref[0, :, f * PIX : f * PIX + HALF] = mirrored[f * OUT_ROWS : (f + 1) * OUT_ROWS]
        out_ref[0, :, f * PIX + HALF : (f + 1) * PIX] = evens[f] - odds[f]


VMEM = pl.BlockSpec(memory_space=pltpu.VMEM)
SMEM = pl.BlockSpec(memory_space=pltpu.SMEM)


def pack(visibility, weights, positions, station_pairs):
    return pl.pallas_call(
        pack_kernel,
        out_shape=jax.ShapeDtypeStruct((SOURCES, 4 * READ_ROWS, LANES), jnp.bfloat16),
        in_specs=[VMEM, VMEM, SMEM, SMEM],
        out_specs=VMEM,
        name="pack",
    )(visibility, weights, positions, station_pairs)


SUMS = (2, FACETS * HALF, HALF)
ROWS_COST = pl.CostEstimate(
    flops=2 * math.prod(SUMS) * BLOCKS * LANES, bytes_accessed=4 * math.prod(SUMS), transcendentals=0
)
TABLE_SCRATCH = pltpu.VMEM((TABLE, BLOCKS, LANES), jnp.float32)
START_SCRATCH = pltpu.VMEM((4, BLOCKS * 8, LANES), jnp.float32)
PANELS = [
    pltpu.VMEM((FACETS * HALF, LANES), jnp.bfloat16),
    pltpu.VMEM((FACETS * HALF, LANES), jnp.bfloat16),
    pltpu.VMEM((HALF, LANES), jnp.bfloat16),
    pltpu.VMEM((HALF, LANES), jnp.bfloat16),
] * BLOCKS
IMAGE_PARAMS = pltpu.CompilerParams(vmem_limit_bytes=48 * 1024 * 1024)


def make_images(half, facet_shift, arrived):
    return pl.pallas_call(
        image_kernel,
        out_shape=jax.ShapeDtypeStruct((PEERS, OUT_ROWS, FACETS * PIX), jnp.bfloat16),
        in_specs=[SMEM, SMEM, VMEM],
        out_specs=VMEM,
        scratch_shapes=[
            TABLE_SCRATCH,
            START_SCRATCH,
            pltpu.VMEM(SUMS, jnp.float32),
            *PANELS,
        ],
        compiler_params=IMAGE_PARAMS,
        cost_estimate=ROWS_COST,
        name="images",
    )(half, facet_shift, arrived)


def combine(scale, place, parts):
    return pl.pallas_call(
        functools.partial(combine_kernel, scale),
        out_shape=jax.ShapeDtypeStruct((1, OUT_ROWS, FACETS * PIX), jnp.float32),
        in_specs=[SMEM, VMEM],
        out_specs=VMEM,
        compiler_params=pltpu.CompilerParams(vmem_limit_bytes=8 * 1024 * 1024),
        name="combine",
    )(place, parts)


def body(visibility, weights, positions, station_pairs, facet_shift):
    half = (lax.axis_index("chan") * HALVES + lax.axis_index("zh")).astype(jnp.int32).reshape(1)
    place = lax.axis_index("x").astype(jnp.int32).reshape(1)
    packed = pack(visibility, weights, positions, station_pairs)
    arrived = lax.all_to_all(packed, ("chan", "zh"), split_axis=0, concat_axis=0, tiled=True)
    images = make_images(half, facet_shift, arrived)
    parts = lax.all_to_all(
        images, ("y", "x"), split_axis=0, concat_axis=0, tiled=True
    )
    scale = 1.0 / math.sqrt(READ_ROWS * GROUPS * 32 * LANES)
    return combine(scale, place, parts)


def solution(mesh):
    fine = Mesh(mesh.devices.reshape(GROUPS, 4, HALVES, 4), ("chan", "y", "zh", "x"))
    line = ("y", "zh", "x")
    in_specs = (
        P(None, ("chan", *line), None),
        P(("chan", *line), None),
        P(),
        P(None, ("chan", *line)),
        P(),
    )
    out_specs = P("chan", line, None)
    return jax.shard_map(body, mesh=fine, in_specs=in_specs, out_specs=out_specs, check_vma=False)
```

```python
import functools
import math

import jax
import jax.numpy as jnp
from jax import lax
from jax.experimental import pallas as pl
from jax.experimental.pallas import tpu as pltpu
from jax.sharding import Mesh, PartitionSpec as P

PIX = 512
HALF = PIX // 2
FACETS = 2
CHANNELS = 1024
GROUPS = 8
LANES = 128
READ_ROWS = 4
RUN_ROWS = 64
RUNS = 4
STEPS = RUN_ROWS // 8
RUN_HALF = RUN_ROWS // 2
HALVES = 2
BLOCKS = GROUPS * READ_ROWS
PEERS = 16
OUT_ROWS = 16
COS_COEF = (
    1.0, -19.739208221435547, 64.93939208984375, -85.45665740966797,
    60.242130279541016, -26.4046688079834, 7.800131797790527, -1.4531123638153076,
)
SIN_COEF = (
    6.2831854820251465, -41.34170150756836, 81.60513305664062, -76.70301818847656,
    42.02592849731445, -14.899847984313965, 3.238137722015381,
)


def poly(coef, z):
    total = jnp.full_like(z, coef[-1])
    for c in coef[-2::-1]:
        total = total * z + c
    return total


def frac(turns):
    return turns - jnp.floor(turns + 0.5)


def cos_sin_reduced(r):
    z = r * r
    return poly(COS_COEF, z), poly(SIN_COEF, z) * r


def cos_sin(turns):
    return cos_sin_reduced(frac(turns))


def pack_kernel(vis_ref, weight_ref, pos_ref, pair_ref, out_ref):
    weight = weight_ref[...].astype(jnp.float32)
    real = vis_ref[0].astype(jnp.float32)
    imag = vis_ref[1].astype(jnp.float32)
    shape = (READ_ROWS, LANES)
    row = lax.broadcasted_iota(jnp.int32, shape, 0)
    lane = lax.broadcasted_iota(jnp.int32, shape, 1)
    spans = jnp.zeros(shape, jnp.float32)
    for axis in range(2):
        rest = jnp.zeros(shape, jnp.float32)
        for b in range(READ_ROWS):
            value = pos_ref[axis, pair_ref[0, b]] - pos_ref[axis, pair_ref[1, b]]
            rest = jnp.where(row == b, value, rest)
        for i in range(3):
            piece = rest.astype(jnp.bfloat16).astype(jnp.float32)
            spans = jnp.where(lane == axis * 3 + i, piece, spans)
            rest = rest - piece
    for g in range(GROUPS):
        lanes = slice(g * LANES, (g + 1) * LANES)
        tile = [real[:, lanes], imag[:, lanes], weight[:, lanes], spans]
        out_ref[g] = jnp.concatenate(tile, axis=0).astype(jnp.bfloat16)


PHASED = 0
WEIGHT, SPANS, C8E, S8E, C8N, S8N, C64N, S64N, TABLE = range(2 * FACETS * RUNS, 2 * FACETS * RUNS + 9)


def rotate(u, turn):
    (ur, ui), (c, s) = u, turn
    return ur * c - ui * s, ur * s + ui * c


def first_kernel(place_ref, shift_ref, data_ref, out_ref, table, starts, *panels):
    for i, sums in enumerate(image_sums(place_ref, shift_ref, data_ref, table, starts, panels)):
        out_ref[i] = sums


def last_kernel(
    place_ref, shift_ref, data_ref, earlier_ref, out_ref, table, starts, acc, *panels
):
    for i, sums in enumerate(image_sums(place_ref, shift_ref, data_ref, table, starts, panels)):
        acc[i] = sums + earlier_ref[i]
    for f in range(FACETS):
        for r in range(RUNS):
            at = (f * RUNS + r) * RUN_HALF
            for i in range(2):
                column = (f * 2 + i) * HALF
                for k in range(RUN_HALF // OUT_ROWS):
                    rows = slice(at + k * OUT_ROWS, at + (k + 1) * OUT_ROWS)
                    rows_imag = slice(at + HALF + k * OUT_ROWS, at + HALF + (k + 1) * OUT_ROWS)
                    a, b = acc[i, rows], acc[i, rows_imag]
                    below, above = (a - b, a + b) if i == 0 else (b + a, b - a)
                    for place, values in ((2 + k, below), (1 - k, above)):
                        chunk = (place % 2) * 8 + r * 2 + place // 2
                        out_ref[chunk, :, column : column + HALF] = values.astype(jnp.bfloat16)


def image_sums(place_ref, shift_ref, data_ref, table, starts, panels):
    for s in range(GROUPS):
        tile = data_ref[s].astype(jnp.float32)
        for a, t in enumerate((PHASED, PHASED + 1, WEIGHT, SPANS)):
            table[t, s * READ_ROWS : (s + 1) * READ_ROWS, :] = tile[
                a * READ_ROWS : (a + 1) * READ_ROWS, :
            ]
    base_row = ((place_ref[0] % HALVES) * RUN_ROWS - HALF).astype(jnp.float32) + (RUN_HALF - 0.5)

    channel = (place_ref[0] // HALVES) * LANES + lax.broadcasted_iota(jnp.int32, (8, LANES), 1)
    frequency = 1.0 + channel.astype(jnp.float32) / CHANNELS
    for i in range(BLOCKS // 8):
        rows = slice(i * 8, (i + 1) * 8)
        spans = table[SPANS, rows, :]
        east, north = (
            (spans[:, a : a + 1] + spans[:, a + 1 : a + 2] + spans[:, a + 2 : a + 3]) * frequency
            for a in (0, 3)
        )
        weight = table[WEIGHT, rows, :]
        seen = weight * table[PHASED, rows, :], weight * table[PHASED + 1, rows, :]
        next_run = cos_sin(east * (2.0 * RUN_ROWS / PIX))
        for f in range(FACETS):
            left = (shift_ref[0, f].astype(jnp.float32) + base_row) * (1.0 / PIX)
            right = (shift_ref[1, f].astype(jnp.float32) - 0.5) * (1.0 / PIX)
            phased = rotate(seen, cos_sin(frac(east * left) + frac(north * right)))
            for r in range(RUNS):
                if r:
                    phased = rotate(phased, next_run)
                at = PHASED + 2 * (f * RUNS + r)
                table[at, rows, :], table[at + 1, rows, :] = phased
        table[C64N, rows, :], table[S64N, rows, :] = cos_sin(north * (64.0 / PIX))
        for place, turns in enumerate((east, north)):
            first = now = cos_sin(turns * (0.5 / PIX))
            step = rotate(first, first)
            twice = 2.0 * step[0]
            before = now[0], -now[1]
            for j in range(8):
                if j:
                    before, now = now, tuple(twice * b - a for a, b in zip(before, now))
                for part in range(2):
                    starts[place * 2 + part, pl.ds(i * 64 + j, 8, stride=8), :] = now[part]
            t = (C8E, C8N)[place]
            table[t, rows, :], table[t + 1, rows, :] = rotate(now, first)

    panels = [panels[i : i + 4] for i in range(0, len(panels), 4)]
    for block, (left_cos, left_sin, right_cos, right_sin) in enumerate(panels):

        def row(i):
            return jnp.broadcast_to(table[i, block : block + 1, :], (8, LANES))

        def put(ref, at, first, second):
            ref[at : at + 16, :] = jnp.concatenate([first, second], axis=0).astype(jnp.bfloat16)

        here = slice(block * 8, (block + 1) * 8)
        base = starts[0, here, :], starts[1, here, :]
        turn = (row(C8E), row(S8E))
        wave = [base, rotate(base, turn)]
        twice = 2.0 * turn[0]
        for _ in range(2, RUN_HALF // 8):
            wave.append(tuple(twice * b - a for a, b in zip(wave[-2], wave[-1])))
        for f in range(FACETS):
            for r in range(RUNS):
                index = PHASED + 2 * (f * RUNS + r)
                real, imag = row(index), row(index + 1)
                at = (f * RUNS + r) * RUN_HALF
                for j in range(0, RUN_HALF // 8, 2):
                    (c0, s0), (c1, s1) = wave[j], wave[j + 1]
                    put(left_cos, at + j * 8, real * c0, real * c1)
                    put(left_cos, at + HALF + j * 8, imag * s0, imag * s1)
                    put(left_sin, at + j * 8, real * s0, real * s1)
                    put(left_sin, at + HALF + j * 8, imag * c0, imag * c1)

        start = starts[2, here, :], starts[3, here, :]
        turn = (row(C8N), row(S8N))
        next_run = (row(C64N), row(S64N))
        anchors = [(start, rotate(start, turn))]
        anchors.append(tuple(rotate(u, next_run) for u in anchors[0]))
        twice = 2.0 * next_run[0]
        for _ in range(2, RUNS):
            anchors.append(
                tuple(
                    tuple(twice * b - a for a, b in zip(old, new))
                    for old, new in zip(anchors[-2], anchors[-1])
                )
            )
        twice = 2.0 * turn[0]
        for r, (first, second) in enumerate(anchors):
            for part, ref in enumerate((right_cos, right_sin)):
                before, now = first[part], second[part]
                for j in range(0, STEPS, 2):
                    if j:
                        before = twice * now - before
                        now = twice * before - now
                    put(ref, r * RUN_ROWS + j * 8, before, now)

    left_cos, left_sin, right_cos, right_sin = (
        jnp.concatenate([ref[...] for ref in refs], axis=1) for refs in zip(*panels)
    )
    contract = (((1,), (1,)), ((), ()))
    for left, right in ((left_cos, right_cos), (left_sin, right_sin)):
        yield lax.dot_general(left, right, contract, preferred_element_type=jnp.float32)


def combine_kernel(scale, place_ref, data_ref, out_ref):
    shape = (OUT_ROWS, PEERS * OUT_ROWS)
    out_row = lax.broadcasted_iota(jnp.int32, shape, 0)
    sent_row = lax.broadcasted_iota(jnp.int32, shape, 1) % OUT_ROWS
    wanted = jnp.where(place_ref[0] < 2, OUT_ROWS - 1 - out_row, out_row)
    pick = (sent_row == wanted).astype(jnp.bfloat16)
    total = jnp.dot(pick, data_ref[...].reshape(PEERS * OUT_ROWS, FACETS * PIX), preferred_element_type=jnp.float32) * scale
    flip = (
        lax.broadcasted_iota(jnp.int32, (HALF, HALF), 0)
        + lax.broadcasted_iota(jnp.int32, (HALF, HALF), 1)
        == HALF - 1
    ).astype(jnp.bfloat16)
    evens = [total[:, f * PIX : f * PIX + HALF] for f in range(FACETS)]
    odds = [total[:, f * PIX + HALF : (f + 1) * PIX] for f in range(FACETS)]
    rest = jnp.concatenate([even + odd for even, odd in zip(evens, odds)], axis=0)
    pieces = []
    for _ in range(3):
        pieces.append(rest.astype(jnp.bfloat16))
        rest = rest - pieces[-1].astype(jnp.float32)
    turned = jnp.dot(jnp.concatenate(pieces, axis=0), flip, preferred_element_type=jnp.float32)
    rows = FACETS * OUT_ROWS
    mirrored = turned[:rows] + turned[rows : 2 * rows] + turned[2 * rows :]
    for f in range(FACETS):
        out_ref[0, :, f * PIX : f * PIX + HALF] = mirrored[f * OUT_ROWS : (f + 1) * OUT_ROWS]
        out_ref[0, :, f * PIX + HALF : (f + 1) * PIX] = evens[f] - odds[f]


VMEM = pl.BlockSpec(memory_space=pltpu.VMEM)
SMEM = pl.BlockSpec(memory_space=pltpu.SMEM)


def pack(visibility, weights, positions, station_pairs):
    return pl.pallas_call(
        pack_kernel,
        out_shape=jax.ShapeDtypeStruct((GROUPS, 4 * READ_ROWS, LANES), jnp.bfloat16),
        in_specs=[VMEM, VMEM, SMEM, SMEM],
        out_specs=VMEM,
        name="pack",
    )(visibility, weights, positions, station_pairs)


SUMS = (2, FACETS * HALF, HALF)
ROWS_COST = pl.CostEstimate(
    flops=2 * math.prod(SUMS) * BLOCKS * LANES, bytes_accessed=4 * math.prod(SUMS), transcendentals=0
)
TABLE_SCRATCH = pltpu.VMEM((TABLE, BLOCKS, LANES), jnp.float32)
START_SCRATCH = pltpu.VMEM((4, BLOCKS * 8, LANES), jnp.float32)
PANELS = [
    pltpu.VMEM((FACETS * HALF, LANES), jnp.bfloat16),
    pltpu.VMEM((FACETS * HALF, LANES), jnp.bfloat16),
    pltpu.VMEM((HALF, LANES), jnp.bfloat16),
    pltpu.VMEM((HALF, LANES), jnp.bfloat16),
] * BLOCKS
IMAGE_PARAMS = pltpu.CompilerParams(vmem_limit_bytes=32 * 1024 * 1024)


def first_sums(half, facet_shift, arrived):
    return pl.pallas_call(
        first_kernel,
        out_shape=jax.ShapeDtypeStruct(SUMS, jnp.float32),
        in_specs=[SMEM, SMEM, VMEM],
        out_specs=VMEM,
        scratch_shapes=[TABLE_SCRATCH, START_SCRATCH, *PANELS],
        compiler_params=IMAGE_PARAMS,
        cost_estimate=ROWS_COST,
        name="first_sums",
    )(half, facet_shift, arrived)


def make_images(half, facet_shift, arrived, earlier):
    return pl.pallas_call(
        last_kernel,
        out_shape=jax.ShapeDtypeStruct((PEERS, OUT_ROWS, FACETS * PIX), jnp.bfloat16),
        in_specs=[SMEM, SMEM, VMEM, VMEM],
        out_specs=VMEM,
        scratch_shapes=[
            TABLE_SCRATCH,
            START_SCRATCH,
            pltpu.VMEM(SUMS, jnp.float32),
            *PANELS,
        ],
        compiler_params=IMAGE_PARAMS,
        cost_estimate=ROWS_COST,
        name="images",
    )(half, facet_shift, arrived, earlier)


def combine(scale, place, parts):
    return pl.pallas_call(
        functools.partial(combine_kernel, scale),
        out_shape=jax.ShapeDtypeStruct((1, OUT_ROWS, FACETS * PIX), jnp.float32),
        in_specs=[SMEM, VMEM],
        out_specs=VMEM,
        compiler_params=pltpu.CompilerParams(vmem_limit_bytes=8 * 1024 * 1024),
        name="combine",
    )(place, parts)


def body(visibility, weights, positions, station_pairs, facet_shift):
    half = (lax.axis_index("chan") * HALVES + lax.axis_index("zh")).astype(jnp.int32).reshape(1)
    place = (2 * lax.axis_index("xh") + lax.axis_index("xl")).astype(jnp.int32).reshape(1)
    packed = pack(visibility, weights, positions, station_pairs)
    own = lax.all_to_all(packed, "chan", split_axis=0, concat_axis=0, tiled=True)
    other = lax.ppermute(own, "zh", [(h, HALVES - 1 - h) for h in range(HALVES)])
    earlier = first_sums(half, facet_shift, own)
    images = make_images(half, facet_shift, other, earlier)
    parts = lax.all_to_all(
        images, ("xl", "y", "xh"), split_axis=0, concat_axis=0, tiled=True
    )
    scale = 1.0 / math.sqrt(READ_ROWS * GROUPS * 32 * LANES)
    return combine(scale, place, parts)


def solution(mesh):
    line = ("y", "zh", "xh", "xl")
    fine = Mesh(mesh.devices.reshape(GROUPS, 4, HALVES, 2, 2), ("chan", *line))
    in_specs = (
        P(None, ("chan", *line), None),
        P(("chan", *line), None),
        P(),
        P(None, ("chan", *line)),
        P(),
    )
    out_specs = P("chan", line, None)
    return jax.shard_map(body, mesh=fine, in_specs=in_specs, out_specs=out_specs, check_vma=False)
```

```python
import functools
import math

import jax
import jax.numpy as jnp
from jax import lax
from jax.experimental import pallas as pl
from jax.experimental.pallas import tpu as pltpu
from jax.sharding import Mesh, PartitionSpec as P

PIX = 512
HALF = PIX // 2
FACETS = 2
CHANNELS = 1024
GROUPS = 8
LANES = 128
READ_ROWS = 4
RUN_ROWS = 64
RUNS = 4
STEPS = RUN_ROWS // 8
RUN_HALF = RUN_ROWS // 2
HALVES = 2
BLOCKS = GROUPS * READ_ROWS
PEERS = 16
OUT_ROWS = 16
COS_COEF = (
    1.0, -19.739208221435547, 64.93939208984375, -85.45665740966797,
    60.242130279541016, -26.4046688079834, 7.800131797790527, -1.4531123638153076,
)
SIN_COEF = (
    6.2831854820251465, -41.34170150756836, 81.60513305664062, -76.70301818847656,
    42.02592849731445, -14.899847984313965, 3.238137722015381,
)


def poly(coef, z):
    total = jnp.full_like(z, coef[-1])
    for c in coef[-2::-1]:
        total = total * z + c
    return total


def frac(turns):
    return turns - jnp.floor(turns + 0.5)


def cos_sin_reduced(r):
    z = r * r
    return poly(COS_COEF, z), poly(SIN_COEF, z) * r


def cos_sin(turns):
    return cos_sin_reduced(frac(turns))


def pack_kernel(vis_ref, weight_ref, pos_ref, pair_ref, out_ref):
    weight = weight_ref[...].astype(jnp.float32)
    real = vis_ref[0].astype(jnp.float32)
    imag = vis_ref[1].astype(jnp.float32)
    shape = (READ_ROWS, LANES)
    row = lax.broadcasted_iota(jnp.int32, shape, 0)
    lane = lax.broadcasted_iota(jnp.int32, shape, 1)
    spans = jnp.zeros(shape, jnp.float32)
    for axis in range(2):
        rest = jnp.zeros(shape, jnp.float32)
        for b in range(READ_ROWS):
            value = pos_ref[axis, pair_ref[0, b]] - pos_ref[axis, pair_ref[1, b]]
            rest = jnp.where(row == b, value, rest)
        for i in range(3):
            piece = rest.astype(jnp.bfloat16).astype(jnp.float32)
            spans = jnp.where(lane == axis * 3 + i, piece, spans)
            rest = rest - piece
    for g in range(GROUPS):
        lanes = slice(g * LANES, (g + 1) * LANES)
        tile = [real[:, lanes], imag[:, lanes], weight[:, lanes], spans]
        out_ref[(g % 2) * (GROUPS // 2) + g // 2] = jnp.concatenate(tile, axis=0).astype(jnp.bfloat16)


PHASED = 0
WEIGHT, SPANS, C8E, S8E, C8N, S8N, C64N, S64N, TABLE = range(2 * FACETS * RUNS, 2 * FACETS * RUNS + 9)


def rotate(u, turn):
    (ur, ui), (c, s) = u, turn
    return ur * c - ui * s, ur * s + ui * c


def first_kernel(place_ref, shift_ref, data_ref, out_ref, table, starts, *panels):
    for i, sums in enumerate(image_sums(place_ref, shift_ref, data_ref, table, starts, panels)):
        out_ref[i] = sums


def last_kernel(
    place_ref, shift_ref, data_ref, earlier_ref, out_ref, table, starts, acc, *panels
):
    for i, sums in enumerate(image_sums(place_ref, shift_ref, data_ref, table, starts, panels)):
        acc[i] = sums + earlier_ref[i]
    for f in range(FACETS):
        for r in range(RUNS):
            at = (f * RUNS + r) * RUN_HALF
            for i in range(2):
                column = (f * 2 + i) * HALF
                for k in range(RUN_HALF // OUT_ROWS):
                    rows = slice(at + k * OUT_ROWS, at + (k + 1) * OUT_ROWS)
                    rows_imag = slice(at + HALF + k * OUT_ROWS, at + HALF + (k + 1) * OUT_ROWS)
                    a, b = acc[i, rows], acc[i, rows_imag]
                    below, above = (a - b, a + b) if i == 0 else (b + a, b - a)
                    for place, values in ((2 + k, below), (1 - k, above)):
                        chunk = (place % 2) * 8 + r * 2 + place // 2
                        out_ref[chunk, :, column : column + HALF] = values.astype(jnp.bfloat16)


def image_sums(place_ref, shift_ref, data_ref, table, starts, panels):
    for s in range(GROUPS):
        tile = data_ref[s].astype(jnp.float32)
        for a, t in enumerate((PHASED, PHASED + 1, WEIGHT, SPANS)):
            table[t, s * READ_ROWS : (s + 1) * READ_ROWS, :] = tile[
                a * READ_ROWS : (a + 1) * READ_ROWS, :
            ]
    base_row = ((place_ref[0] % HALVES) * RUN_ROWS - HALF).astype(jnp.float32) + (RUN_HALF - 0.5)

    channel = (place_ref[0] // HALVES) * LANES + lax.broadcasted_iota(jnp.int32, (8, LANES), 1)
    frequency = 1.0 + channel.astype(jnp.float32) / CHANNELS
    for i in range(BLOCKS // 8):
        rows = slice(i * 8, (i + 1) * 8)
        spans = table[SPANS, rows, :]
        east, north = (
            (spans[:, a : a + 1] + spans[:, a + 1 : a + 2] + spans[:, a + 2 : a + 3]) * frequency
            for a in (0, 3)
        )
        weight = table[WEIGHT, rows, :]
        seen = weight * table[PHASED, rows, :], weight * table[PHASED + 1, rows, :]
        next_run = cos_sin(east * (2.0 * RUN_ROWS / PIX))
        for f in range(FACETS):
            left = (shift_ref[0, f].astype(jnp.float32) + base_row) * (1.0 / PIX)
            right = (shift_ref[1, f].astype(jnp.float32) - 0.5) * (1.0 / PIX)
            phased = rotate(seen, cos_sin(frac(east * left) + frac(north * right)))
            for r in range(RUNS):
                if r:
                    phased = rotate(phased, next_run)
                at = PHASED + 2 * (f * RUNS + r)
                table[at, rows, :], table[at + 1, rows, :] = phased
        table[C64N, rows, :], table[S64N, rows, :] = cos_sin(north * (64.0 / PIX))
        for place, turns in enumerate((east, north)):
            first = now = cos_sin(turns * (0.5 / PIX))
            step = rotate(first, first)
            twice = 2.0 * step[0]
            before = now[0], -now[1]
            for j in range(8):
                if j:
                    before, now = now, tuple(twice * b - a for a, b in zip(before, now))
                for part in range(2):
                    starts[place * 2 + part, pl.ds(i * 64 + j, 8, stride=8), :] = now[part]
            t = (C8E, C8N)[place]
            table[t, rows, :], table[t + 1, rows, :] = rotate(now, first)

    panels = [panels[i : i + 4] for i in range(0, len(panels), 4)]
    for block, (left_cos, left_sin, right_cos, right_sin) in enumerate(panels):

        def row(i):
            return jnp.broadcast_to(table[i, block : block + 1, :], (8, LANES))

        def put(ref, at, first, second):
            ref[at : at + 16, :] = jnp.concatenate([first, second], axis=0).astype(jnp.bfloat16)

        here = slice(block * 8, (block + 1) * 8)
        base = starts[0, here, :], starts[1, here, :]
        turn = (row(C8E), row(S8E))
        wave = [base, rotate(base, turn)]
        twice = 2.0 * turn[0]
        for _ in range(2, RUN_HALF // 8):
            wave.append(tuple(twice * b - a for a, b in zip(wave[-2], wave[-1])))
        for f in range(FACETS):
            for r in range(RUNS):
                index = PHASED + 2 * (f * RUNS + r)
                real, imag = row(index), row(index + 1)
                at = (f * RUNS + r) * RUN_HALF
                for j in range(0, RUN_HALF // 8, 2):
                    (c0, s0), (c1, s1) = wave[j], wave[j + 1]
                    put(left_cos, at + j * 8, real * c0, real * c1)
                    put(left_cos, at + HALF + j * 8, imag * s0, imag * s1)
                    put(left_sin, at + j * 8, real * s0, real * s1)
                    put(left_sin, at + HALF + j * 8, imag * c0, imag * c1)

        start = starts[2, here, :], starts[3, here, :]
        turn = (row(C8N), row(S8N))
        next_run = (row(C64N), row(S64N))
        anchors = [(start, rotate(start, turn))]
        anchors.append(tuple(rotate(u, next_run) for u in anchors[0]))
        twice = 2.0 * next_run[0]
        for _ in range(2, RUNS):
            anchors.append(
                tuple(
                    tuple(twice * b - a for a, b in zip(old, new))
                    for old, new in zip(anchors[-2], anchors[-1])
                )
            )
        twice = 2.0 * turn[0]
        for r, (first, second) in enumerate(anchors):
            for part, ref in enumerate((right_cos, right_sin)):
                before, now = first[part], second[part]
                for j in range(0, STEPS, 2):
                    if j:
                        before = twice * now - before
                        now = twice * before - now
                    put(ref, r * RUN_ROWS + j * 8, before, now)

    left_cos, left_sin, right_cos, right_sin = (
        jnp.concatenate([ref[...] for ref in refs], axis=1) for refs in zip(*panels)
    )
    contract = (((1,), (1,)), ((), ()))
    for left, right in ((left_cos, right_cos), (left_sin, right_sin)):
        yield lax.dot_general(left, right, contract, preferred_element_type=jnp.float32)


def combine_kernel(scale, place_ref, data_ref, out_ref):
    shape = (OUT_ROWS, PEERS * OUT_ROWS)
    out_row = lax.broadcasted_iota(jnp.int32, shape, 0)
    sent_row = lax.broadcasted_iota(jnp.int32, shape, 1) % OUT_ROWS
    wanted = jnp.where(place_ref[0] < 2, OUT_ROWS - 1 - out_row, out_row)
    pick = (sent_row == wanted).astype(jnp.bfloat16)
    total = jnp.dot(pick, data_ref[...].reshape(PEERS * OUT_ROWS, FACETS * PIX), preferred_element_type=jnp.float32) * scale
    flip = (
        lax.broadcasted_iota(jnp.int32, (HALF, HALF), 0)
        + lax.broadcasted_iota(jnp.int32, (HALF, HALF), 1)
        == HALF - 1
    ).astype(jnp.bfloat16)
    evens = [total[:, f * PIX : f * PIX + HALF] for f in range(FACETS)]
    odds = [total[:, f * PIX + HALF : (f + 1) * PIX] for f in range(FACETS)]
    rest = jnp.concatenate([even + odd for even, odd in zip(evens, odds)], axis=0)
    pieces = []
    for _ in range(3):
        pieces.append(rest.astype(jnp.bfloat16))
        rest = rest - pieces[-1].astype(jnp.float32)
    turned = jnp.dot(jnp.concatenate(pieces, axis=0), flip, preferred_element_type=jnp.float32)
    rows = FACETS * OUT_ROWS
    mirrored = turned[:rows] + turned[rows : 2 * rows] + turned[2 * rows :]
    for f in range(FACETS):
        out_ref[0, :, f * PIX : f * PIX + HALF] = mirrored[f * OUT_ROWS : (f + 1) * OUT_ROWS]
        out_ref[0, :, f * PIX + HALF : (f + 1) * PIX] = evens[f] - odds[f]


VMEM = pl.BlockSpec(memory_space=pltpu.VMEM)
SMEM = pl.BlockSpec(memory_space=pltpu.SMEM)


def pack(visibility, weights, positions, station_pairs):
    return pl.pallas_call(
        pack_kernel,
        out_shape=jax.ShapeDtypeStruct((GROUPS, 4 * READ_ROWS, LANES), jnp.bfloat16),
        in_specs=[VMEM, VMEM, SMEM, SMEM],
        out_specs=VMEM,
        name="pack",
    )(visibility, weights, positions, station_pairs)


SUMS = (2, FACETS * HALF, HALF)
ROWS_COST = pl.CostEstimate(
    flops=2 * math.prod(SUMS) * BLOCKS * LANES, bytes_accessed=4 * math.prod(SUMS), transcendentals=0
)
TABLE_SCRATCH = pltpu.VMEM((TABLE, BLOCKS, LANES), jnp.float32)
START_SCRATCH = pltpu.VMEM((4, BLOCKS * 8, LANES), jnp.float32)
PANELS = [
    pltpu.VMEM((FACETS * HALF, LANES), jnp.bfloat16),
    pltpu.VMEM((FACETS * HALF, LANES), jnp.bfloat16),
    pltpu.VMEM((HALF, LANES), jnp.bfloat16),
    pltpu.VMEM((HALF, LANES), jnp.bfloat16),
] * BLOCKS
IMAGE_PARAMS = pltpu.CompilerParams(vmem_limit_bytes=32 * 1024 * 1024)


def first_sums(half, facet_shift, arrived):
    return pl.pallas_call(
        first_kernel,
        out_shape=jax.ShapeDtypeStruct(SUMS, jnp.float32),
        in_specs=[SMEM, SMEM, VMEM],
        out_specs=VMEM,
        scratch_shapes=[TABLE_SCRATCH, START_SCRATCH, *PANELS],
        compiler_params=IMAGE_PARAMS,
        cost_estimate=ROWS_COST,
        name="first_sums",
    )(half, facet_shift, arrived)


def make_images(half, facet_shift, arrived, earlier):
    return pl.pallas_call(
        last_kernel,
        out_shape=jax.ShapeDtypeStruct((PEERS, OUT_ROWS, FACETS * PIX), jnp.bfloat16),
        in_specs=[SMEM, SMEM, VMEM, VMEM],
        out_specs=VMEM,
        scratch_shapes=[
            TABLE_SCRATCH,
            START_SCRATCH,
            pltpu.VMEM(SUMS, jnp.float32),
            *PANELS,
        ],
        compiler_params=IMAGE_PARAMS,
        cost_estimate=ROWS_COST,
        name="images",
    )(half, facet_shift, arrived, earlier)


def combine(scale, place, parts):
    return pl.pallas_call(
        functools.partial(combine_kernel, scale),
        out_shape=jax.ShapeDtypeStruct((1, OUT_ROWS, FACETS * PIX), jnp.float32),
        in_specs=[SMEM, VMEM],
        out_specs=VMEM,
        compiler_params=pltpu.CompilerParams(vmem_limit_bytes=8 * 1024 * 1024),
        name="combine",
    )(place, parts)


def body(visibility, weights, positions, station_pairs, facet_shift):
    half = (lax.axis_index(("zl", "core")) * HALVES + lax.axis_index("zh")).astype(jnp.int32).reshape(1)
    place = (2 * lax.axis_index("xh") + lax.axis_index("xl")).astype(jnp.int32).reshape(1)
    packed = pack(visibility, weights, positions, station_pairs)
    own = lax.all_to_all(packed, ("core", "zl"), split_axis=0, concat_axis=0, tiled=True)
    other = lax.ppermute(own, "zh", [(h, HALVES - 1 - h) for h in range(HALVES)])
    earlier = first_sums(half, facet_shift, own)
    images = make_images(half, facet_shift, other, earlier)
    parts = lax.all_to_all(
        images, ("xl", "y", "xh"), split_axis=0, concat_axis=0, tiled=True
    )
    scale = 1.0 / math.sqrt(READ_ROWS * GROUPS * 32 * LANES)
    return combine(scale, place, parts)


def solution(mesh):
    line = ("y", "zh", "xh", "xl")
    fine = Mesh(mesh.devices.reshape(GROUPS // 2, 2, 4, HALVES, 2, 2), ("zl", "core", *line))
    in_specs = (
        P(None, ("zl", "core", *line), None),
        P(("zl", "core", *line), None),
        P(),
        P(None, ("zl", "core", *line)),
        P(),
    )
    out_specs = P(("zl", "core"), line, None)
    return jax.shard_map(body, mesh=fine, in_specs=in_specs, out_specs=out_specs, check_vma=False)
```

```python
import functools
import math

import jax
import jax.numpy as jnp
from jax import lax
from jax.experimental import pallas as pl
from jax.experimental.pallas import tpu as pltpu
from jax.sharding import Mesh, PartitionSpec as P

PIX = 512
HALF = PIX // 2
FACETS = 2
CHANNELS = 1024
GROUPS = 8
LANES = 128
READ_ROWS = 4
RUN_ROWS = 64
RUNS = 4
STEPS = RUN_ROWS // 8
RUN_HALF = RUN_ROWS // 2
HALVES = 2
BLOCKS = GROUPS * READ_ROWS
PEERS = 16
OUT_ROWS = 16
COS_COEF = (
    1.0, -19.739208221435547, 64.93939208984375, -85.45665740966797,
    60.242130279541016, -26.4046688079834, 7.800131797790527, -1.4531123638153076,
)
SIN_COEF = (
    6.2831854820251465, -41.34170150756836, 81.60513305664062, -76.70301818847656,
    42.02592849731445, -14.899847984313965, 3.238137722015381,
)


def poly(coef, z):
    total = jnp.full_like(z, coef[-1])
    for c in coef[-2::-1]:
        total = total * z + c
    return total


def frac(turns):
    return turns - jnp.floor(turns + 0.5)


def cos_sin_reduced(r):
    z = r * r
    return poly(COS_COEF, z), poly(SIN_COEF, z) * r


def cos_sin(turns):
    return cos_sin_reduced(frac(turns))


def pack_kernel(vis_ref, weight_ref, pos_ref, pair_ref, out_ref):
    weight = weight_ref[...].astype(jnp.float32)
    real = vis_ref[0].astype(jnp.float32)
    imag = vis_ref[1].astype(jnp.float32)
    shape = (READ_ROWS, LANES)
    row = lax.broadcasted_iota(jnp.int32, shape, 0)
    lane = lax.broadcasted_iota(jnp.int32, shape, 1)
    spans = jnp.zeros(shape, jnp.float32)
    for axis in range(2):
        rest = jnp.zeros(shape, jnp.float32)
        for b in range(READ_ROWS):
            value = pos_ref[axis, pair_ref[0, b]] - pos_ref[axis, pair_ref[1, b]]
            rest = jnp.where(row == b, value, rest)
        for i in range(3):
            piece = rest.astype(jnp.bfloat16).astype(jnp.float32)
            spans = jnp.where(lane == axis * 3 + i, piece, spans)
            rest = rest - piece
    for g in range(GROUPS):
        lanes = slice(g * LANES, (g + 1) * LANES)
        tile = [real[:, lanes], imag[:, lanes], weight[:, lanes], spans]
        out_ref[g] = jnp.concatenate(tile, axis=0).astype(jnp.bfloat16)


PHASED = 0
WEIGHT, SPANS, C8E, S8E, C8N, S8N, C64N, S64N, TABLE = range(2 * FACETS * RUNS, 2 * FACETS * RUNS + 9)


def rotate(u, turn):
    (ur, ui), (c, s) = u, turn
    return ur * c - ui * s, ur * s + ui * c


def first_kernel(place_ref, shift_ref, data_ref, out_ref, table, starts, *panels):
    for i, sums in enumerate(image_sums(place_ref, shift_ref, data_ref, table, starts, panels)):
        out_ref[i] = sums


def last_kernel(
    place_ref, shift_ref, data_ref, earlier_ref, out_ref, table, starts, acc, *panels
):
    for i, sums in enumerate(image_sums(place_ref, shift_ref, data_ref, table, starts, panels)):
        acc[i] = sums + earlier_ref[i]
    for f in range(FACETS):
        for r in range(RUNS):
            at = (f * RUNS + r) * RUN_HALF
            for i in range(2):
                column = (f * 2 + i) * HALF
                for k in range(RUN_HALF // OUT_ROWS):
                    rows = slice(at + k * OUT_ROWS, at + (k + 1) * OUT_ROWS)
                    rows_imag = slice(at + HALF + k * OUT_ROWS, at + HALF + (k + 1) * OUT_ROWS)
                    a, b = acc[i, rows], acc[i, rows_imag]
                    below, above = (a - b, a + b) if i == 0 else (b + a, b - a)
                    for place, values in ((2 + k, below), (1 - k, above)):
                        chunk = place % 2 * 8 + r % 2 * 4 + place // 2 * 2 + r // 2
                        out_ref[chunk, :, column : column + HALF] = values.astype(jnp.bfloat16)


def image_sums(place_ref, shift_ref, data_ref, table, starts, panels):
    for s in range(GROUPS):
        tile = data_ref[s].astype(jnp.float32)
        for a, t in enumerate((PHASED, PHASED + 1, WEIGHT, SPANS)):
            table[t, s * READ_ROWS : (s + 1) * READ_ROWS, :] = tile[
                a * READ_ROWS : (a + 1) * READ_ROWS, :
            ]
    base_row = ((place_ref[0] % HALVES) * RUN_ROWS - HALF).astype(jnp.float32) + (RUN_HALF - 0.5)

    channel = (place_ref[0] // HALVES) * LANES + lax.broadcasted_iota(jnp.int32, (8, LANES), 1)
    frequency = 1.0 + channel.astype(jnp.float32) / CHANNELS
    for i in range(BLOCKS // 8):
        rows = slice(i * 8, (i + 1) * 8)
        spans = table[SPANS, rows, :]
        east, north = (
            (spans[:, a : a + 1] + spans[:, a + 1 : a + 2] + spans[:, a + 2 : a + 3]) * frequency
            for a in (0, 3)
        )
        weight = table[WEIGHT, rows, :]
        seen = weight * table[PHASED, rows, :], weight * table[PHASED + 1, rows, :]
        next_run = cos_sin(east * (2.0 * RUN_ROWS / PIX))
        for f in range(FACETS):
            left = (shift_ref[0, f].astype(jnp.float32) + base_row) * (1.0 / PIX)
            right = (shift_ref[1, f].astype(jnp.float32) - 0.5) * (1.0 / PIX)
            phased = rotate(seen, cos_sin(frac(east * left) + frac(north * right)))
            for r in range(RUNS):
                if r:
                    phased = rotate(phased, next_run)
                at = PHASED + 2 * (f * RUNS + r)
                table[at, rows, :], table[at + 1, rows, :] = phased
        table[C64N, rows, :], table[S64N, rows, :] = cos_sin(north * (64.0 / PIX))
        for place, turns in enumerate((east, north)):
            first = now = cos_sin(turns * (0.5 / PIX))
            step = rotate(first, first)
            twice = 2.0 * step[0]
            before = now[0], -now[1]
            for j in range(8):
                if j:
                    before, now = now, tuple(twice * b - a for a, b in zip(before, now))
                for part in range(2):
                    starts[place * 2 + part, pl.ds(i * 64 + j, 8, stride=8), :] = now[part]
            t = (C8E, C8N)[place]
            table[t, rows, :], table[t + 1, rows, :] = rotate(now, first)

    panels = [panels[i : i + 4] for i in range(0, len(panels), 4)]
    for block, (left_cos, left_sin, right_cos, right_sin) in enumerate(panels):

        def row(i):
            return jnp.broadcast_to(table[i, block : block + 1, :], (8, LANES))

        def put(ref, at, first, second):
            ref[at : at + 16, :] = jnp.concatenate([first, second], axis=0).astype(jnp.bfloat16)

        here = slice(block * 8, (block + 1) * 8)
        base = starts[0, here, :], starts[1, here, :]
        turn = (row(C8E), row(S8E))
        wave = [base, rotate(base, turn)]
        twice = 2.0 * turn[0]
        for _ in range(2, RUN_HALF // 8):
            wave.append(tuple(twice * b - a for a, b in zip(wave[-2], wave[-1])))
        for f in range(FACETS):
            for r in range(RUNS):
                index = PHASED + 2 * (f * RUNS + r)
                real, imag = row(index), row(index + 1)
                at = (f * RUNS + r) * RUN_HALF
                for j in range(0, RUN_HALF // 8, 2):
                    (c0, s0), (c1, s1) = wave[j], wave[j + 1]
                    put(left_cos, at + j * 8, real * c0, real * c1)
                    put(left_cos, at + HALF + j * 8, imag * s0, imag * s1)
                    put(left_sin, at + j * 8, real * s0, real * s1)
                    put(left_sin, at + HALF + j * 8, imag * c0, imag * c1)

        start = starts[2, here, :], starts[3, here, :]
        turn = (row(C8N), row(S8N))
        next_run = (row(C64N), row(S64N))
        anchors = [(start, rotate(start, turn))]
        anchors.append(tuple(rotate(u, next_run) for u in anchors[0]))
        twice = 2.0 * next_run[0]
        for _ in range(2, RUNS):
            anchors.append(
                tuple(
                    tuple(twice * b - a for a, b in zip(old, new))
                    for old, new in zip(anchors[-2], anchors[-1])
                )
            )
        twice = 2.0 * turn[0]
        for r, (first, second) in enumerate(anchors):
            for part, ref in enumerate((right_cos, right_sin)):
                before, now = first[part], second[part]
                for j in range(0, STEPS, 2):
                    if j:
                        before = twice * now - before
                        now = twice * before - now
                    put(ref, r * RUN_ROWS + j * 8, before, now)

    left_cos, left_sin, right_cos, right_sin = (
        jnp.concatenate([ref[...] for ref in refs], axis=1) for refs in zip(*panels)
    )
    contract = (((1,), (1,)), ((), ()))
    for left, right in ((left_cos, right_cos), (left_sin, right_sin)):
        yield lax.dot_general(left, right, contract, preferred_element_type=jnp.float32)


def combine_kernel(scale, place_ref, data_ref, out_ref):
    shape = (OUT_ROWS, PEERS * OUT_ROWS)
    out_row = lax.broadcasted_iota(jnp.int32, shape, 0)
    sent_row = lax.broadcasted_iota(jnp.int32, shape, 1) % OUT_ROWS
    wanted = jnp.where(place_ref[0] < 2, OUT_ROWS - 1 - out_row, out_row)
    pick = (sent_row == wanted).astype(jnp.bfloat16)
    total = jnp.dot(pick, data_ref[...].reshape(PEERS * OUT_ROWS, FACETS * PIX), preferred_element_type=jnp.float32) * scale
    flip = (
        lax.broadcasted_iota(jnp.int32, (HALF, HALF), 0)
        + lax.broadcasted_iota(jnp.int32, (HALF, HALF), 1)
        == HALF - 1
    ).astype(jnp.bfloat16)
    evens = [total[:, f * PIX : f * PIX + HALF] for f in range(FACETS)]
    odds = [total[:, f * PIX + HALF : (f + 1) * PIX] for f in range(FACETS)]
    rest = jnp.concatenate([even + odd for even, odd in zip(evens, odds)], axis=0)
    pieces = []
    for _ in range(3):
        pieces.append(rest.astype(jnp.bfloat16))
        rest = rest - pieces[-1].astype(jnp.float32)
    turned = jnp.dot(jnp.concatenate(pieces, axis=0), flip, preferred_element_type=jnp.float32)
    rows = FACETS * OUT_ROWS
    mirrored = turned[:rows] + turned[rows : 2 * rows] + turned[2 * rows :]
    for f in range(FACETS):
        out_ref[0, :, f * PIX : f * PIX + HALF] = mirrored[f * OUT_ROWS : (f + 1) * OUT_ROWS]
        out_ref[0, :, f * PIX + HALF : (f + 1) * PIX] = evens[f] - odds[f]


VMEM = pl.BlockSpec(memory_space=pltpu.VMEM)
SMEM = pl.BlockSpec(memory_space=pltpu.SMEM)


def pack(visibility, weights, positions, station_pairs):
    return pl.pallas_call(
        pack_kernel,
        out_shape=jax.ShapeDtypeStruct((GROUPS, 4 * READ_ROWS, LANES), jnp.bfloat16),
        in_specs=[VMEM, VMEM, SMEM, SMEM],
        out_specs=VMEM,
        name="pack",
    )(visibility, weights, positions, station_pairs)


SUMS = (2, FACETS * HALF, HALF)
ROWS_COST = pl.CostEstimate(
    flops=2 * math.prod(SUMS) * BLOCKS * LANES, bytes_accessed=4 * math.prod(SUMS), transcendentals=0
)
TABLE_SCRATCH = pltpu.VMEM((TABLE, BLOCKS, LANES), jnp.float32)
START_SCRATCH = pltpu.VMEM((4, BLOCKS * 8, LANES), jnp.float32)
PANELS = [
    pltpu.VMEM((FACETS * HALF, LANES), jnp.bfloat16),
    pltpu.VMEM((FACETS * HALF, LANES), jnp.bfloat16),
    pltpu.VMEM((HALF, LANES), jnp.bfloat16),
    pltpu.VMEM((HALF, LANES), jnp.bfloat16),
] * BLOCKS
IMAGE_PARAMS = pltpu.CompilerParams(vmem_limit_bytes=32 * 1024 * 1024)


def first_sums(half, facet_shift, arrived):
    return pl.pallas_call(
        first_kernel,
        out_shape=jax.ShapeDtypeStruct(SUMS, jnp.float32),
        in_specs=[SMEM, SMEM, VMEM],
        out_specs=VMEM,
        scratch_shapes=[TABLE_SCRATCH, START_SCRATCH, *PANELS],
        compiler_params=IMAGE_PARAMS,
        cost_estimate=ROWS_COST,
        name="first_sums",
    )(half, facet_shift, arrived)


def make_images(half, facet_shift, arrived, earlier):
    return pl.pallas_call(
        last_kernel,
        out_shape=jax.ShapeDtypeStruct((PEERS, OUT_ROWS, FACETS * PIX), jnp.bfloat16),
        in_specs=[SMEM, SMEM, VMEM, VMEM],
        out_specs=VMEM,
        scratch_shapes=[
            TABLE_SCRATCH,
            START_SCRATCH,
            pltpu.VMEM(SUMS, jnp.float32),
            *PANELS,
        ],
        compiler_params=IMAGE_PARAMS,
        cost_estimate=ROWS_COST,
        name="images",
    )(half, facet_shift, arrived, earlier)


def combine(scale, place, parts):
    return pl.pallas_call(
        functools.partial(combine_kernel, scale),
        out_shape=jax.ShapeDtypeStruct((1, OUT_ROWS, FACETS * PIX), jnp.float32),
        in_specs=[SMEM, VMEM],
        out_specs=VMEM,
        compiler_params=pltpu.CompilerParams(vmem_limit_bytes=8 * 1024 * 1024),
        name="combine",
    )(place, parts)


def body(visibility, weights, positions, station_pairs, facet_shift):
    half = (lax.axis_index("chan") * HALVES + lax.axis_index("zh")).astype(jnp.int32).reshape(1)
    place = (2 * lax.axis_index("xh") + lax.axis_index("xl")).astype(jnp.int32).reshape(1)
    packed = pack(visibility, weights, positions, station_pairs)
    own = lax.all_to_all(packed, "chan", split_axis=0, concat_axis=0, tiled=True)
    other = lax.ppermute(own, "zh", [(h, HALVES - 1 - h) for h in range(HALVES)])
    earlier = first_sums(half, facet_shift, own)
    images = make_images(half, facet_shift, other, earlier)
    parts = lax.all_to_all(
        images, ("xl", "yl", "xh", "yh"), split_axis=0, concat_axis=0, tiled=True
    )
    scale = 1.0 / math.sqrt(READ_ROWS * GROUPS * 32 * LANES)
    return combine(scale, place, parts)


def solution(mesh):
    line = ("yh", "yl", "zh", "xh", "xl")
    fine = Mesh(mesh.devices.reshape(GROUPS, 2, 2, HALVES, 2, 2), ("chan", *line))
    in_specs = (
        P(None, ("chan", *line), None),
        P(("chan", *line), None),
        P(),
        P(None, ("chan", *line)),
        P(),
    )
    out_specs = P("chan", line, None)
    return jax.shard_map(body, mesh=fine, in_specs=in_specs, out_specs=out_specs, check_vma=False)
```
